128 devices in a mesh: group: 8 (over y, core), sub: 16 (over z, x).
Axes of the slice: x: 4, y: 4, z: 4, core: 2. Of those that a mesh axis runs over, the one named last changes fastest.
Arguments:
- shared_sizes: int32 [8, 16, 2], P('group', 'sub'), may hold values from 0 to 256, as said below
- stiffness: float32 [8, 16], P('group', 'sub'), may hold values from 0.1 to 10
- load_cases: float32 [8, 16, 1024, 384], P('group', 'sub'), may hold values from -6 to 6
- schur_blocks: bfloat16 [8, 16, 1024, 1024], P('group', 'sub')
- neumann_inverse: bfloat16 [8, 16, 1024, 1024], P('group', 'sub')
- coarse_basis: bfloat16 [8, 16, 32, 1024], P('group', 'sub'), may hold values from -0.1875 to 0.1875
- coarse_dofs: int32 [8, 16, 32], P('group', 'sub'), may hold values from 0 to 2047
- coarse_inverse: float32 [2048, 2048], P('sub'), as said below
Outputs:
- solution: float32 [8, 16, 1024, 384], P('group', 'sub')
- residual: float32 [8, 16, 1024, 384], P('group', 'sub')
The draws below stay inside these ranges and needn't reach their ends.
Inputs may be any that keep to these rules, and one draw needn't show every extreme that they name: shared_sizes[g, s, 0] equals shared_sizes[g, s - 1, 1]; the lower share of the first and the upper share of the last subdomain of a group are 0, the other shares lie in 128 to 256, and in every group some subdomain shares exactly 256 with its upper neighbour. `coarse_inverse`: symmetric.
All inputs are finite; a program needn't handle non-finite values.
Results may differ from the reference program's by a relative error of at most 0.0075.
Values sent between devices are 32-bit elements; how exact they have to be, the bound alone decides.
A program may use at most 128 MiB of HBM per device.

```python
import math
import jax
import jax.numpy as jnp
from jax import lax

NI = 1024
CASES = 384
MAXSH = 256
NCL = 32
ITERS = 4
NC = 2048
N_GROUP = 8
N_SUB = 16


def operator_pair(key):
    key_diag, key_off = jax.random.split(jax.random.fold_in(key, 11))
    diagonal = jax.random.uniform(key_diag, (N_GROUP, N_SUB, NI), jnp.float32, 0.8, 1.6)
    perturb = jax.random.normal(key_off, (N_GROUP, N_SUB, NI, NI), jnp.float32) * (0.25 / math.sqrt(NI))
    perturb = (perturb + jnp.swapaxes(perturb, 2, 3)) * (1.0 / math.sqrt(2.0))
    identity = jnp.eye(NI, dtype=jnp.float32)
    inverse = 1.0 / diagonal
    schur = diagonal[..., :, None] * identity + perturb
    neumann = inverse[..., :, None] * identity - inverse[..., :, None] * perturb * inverse[..., None, :]
    return (schur, neumann)


def draw_schur_blocks(key, part):
    return operator_pair(key)[0].astype(jnp.bfloat16)


def draw_neumann_inverse(key, part):
    return operator_pair(key)[1].astype(jnp.bfloat16)


def draw_shared_sizes(key, part):
    key_size, key_peak = jax.random.split(jax.random.fold_in(key, 23))
    upper = jax.random.randint(key_size, (N_GROUP, N_SUB), MAXSH // 2, MAXSH + 1)
    peak_at = jax.random.randint(key_peak, (N_GROUP, 1), 0, N_SUB - 1)
    position = jnp.arange(N_SUB)[None, :]
    upper = jnp.where(position == peak_at, MAXSH, upper)
    upper = jnp.where(position == N_SUB - 1, 0, upper)
    lower = jnp.concatenate([jnp.zeros((N_GROUP, 1), upper.dtype), upper[:, :-1]], axis=1)
    return jnp.stack([lower, upper], axis=-1).astype(jnp.int32)


def draw_coarse_inverse(key, part):
    perturb = jax.random.normal(jax.random.fold_in(key, 37), (NC, NC), jnp.float32) * (0.25 / math.sqrt(NC))
    perturb = (perturb + perturb.T) * (1.0 / math.sqrt(2.0))
    return jnp.eye(NC, dtype=jnp.float32) + perturb


def plant(array, stream_key, low, top_value):
    index_at = [jax.random.randint(jax.random.fold_in(stream_key, axis), (), 0, length) for axis, length in enumerate(array.shape)]
    widest = array.shape.index(max(array.shape))
    neighbour = index_at[:widest] + [(index_at[widest] + 1) % array.shape[widest]] + index_at[widest + 1:]
    return array.at[tuple(index_at)].set(low).at[tuple(neighbour)].set(top_value)


def level_of(rng, extent, cuts, smallest, high):
    gain, own = 1.0, jax.random.fold_in(rng, 6)
    for dim, parts in cuts:
        heights = jnp.exp(jax.random.uniform(jax.random.fold_in(own, dim), (parts,), jnp.float32, smallest / len(cuts), high / len(cuts)))
        gain = gain * jnp.repeat(heights, extent[dim] // parts).reshape([-1 if axis == dim else 1 for axis in range(len(extent))])
    return gain


def centred(key, shape, width, bound, cuts=(), held_as=jnp.bfloat16):
    drawn = width * jax.random.normal(key, shape, jnp.float32)
    if cuts:
        drawn = drawn * level_of(key, shape, cuts, -0.22, 0.18)
    return jnp.clip(drawn, -bound, bound).astype(held_as)


def setup_inputs(seed: int = 0) -> dict:
    splits = jax.random.split(jax.random.key(seed), 9)
    return {
        "shared_sizes": draw_shared_sizes(jax.random.fold_in(splits[8], 71), 0),
        "stiffness": jnp.clip(jnp.exp(math.log(10.0) - 4.6051702 * jax.random.uniform(splits[1], (N_GROUP, N_SUB), jnp.float32) ** level_of(splits[1], (N_GROUP, N_SUB), ((0, 8), (1, 16)), -0.2, 0.2)), 0.1, 10.0),
        "load_cases": centred(splits[2], (N_GROUP, N_SUB, NI, CASES), 1.0, 6.0, ((0, 8), (1, 16)), jnp.float32),
        "schur_blocks": draw_schur_blocks(jax.random.fold_in(splits[8], 71), 0),
        "neumann_inverse": draw_neumann_inverse(jax.random.fold_in(splits[8], 71), 0),
        "coarse_basis": centred(splits[5], (N_GROUP, N_SUB, NCL, NI), (NI ** -0.5), 0.1875, ((0, 8), (1, 16))),
        "coarse_dofs": plant(jax.random.randint(splits[6], (N_GROUP, N_SUB, NCL), 0, NC), jax.random.fold_in(splits[6], 1), 0, NC - 1).astype(jnp.int32),
        "coarse_inverse": draw_coarse_inverse(jax.random.fold_in(splits[8], 71), 0),
    }


OMEGA = 0.6


def lift_piece(tail_rows, share_size):
    slab_width = tail_rows.shape[0]
    rolled = jnp.roll(tail_rows, share_size - slab_width, axis=0)
    inside = (jnp.arange(slab_width) < share_size)[:, None]
    return jnp.where(inside, rolled, jnp.zeros_like(rolled))


def place_piece(head_rows, share_size):
    slab_width = head_rows.shape[0]
    inside = (jnp.arange(slab_width) < share_size)[:, None]
    masked = jnp.where(inside, head_rows, jnp.zeros_like(head_rows))
    return jnp.roll(masked, slab_width - share_size, axis=0)


def assemble(vector, shared_sizes):
    tail_rows = vector[:, :, NI - MAXSH:]
    head_rows = vector[:, :, :MAXSH]
    lifted = jax.vmap(jax.vmap(lift_piece))(tail_rows, shared_sizes[:, :, 1])
    from_lower = jnp.concatenate([jnp.zeros_like(lifted[:, :1]), lifted[:, :-1]], axis=1)
    from_upper = jnp.concatenate([head_rows[:, 1:], jnp.zeros_like(head_rows[:, :1])], axis=1)
    placed = jax.vmap(jax.vmap(place_piece))(from_upper, shared_sizes[:, :, 1])
    return jnp.concatenate([head_rows + from_lower, vector[:, :, MAXSH:NI - MAXSH], tail_rows + placed], axis=2)


def interface_weights(shared_sizes, stiffness):
    nothing = jnp.zeros_like(stiffness[:, :1])
    lower = jnp.concatenate([nothing, stiffness[:, :-1]], axis=1)
    upper = jnp.concatenate([stiffness[:, 1:], nothing], axis=1)
    low_weight = stiffness / (stiffness + lower)
    up_weight = stiffness / (stiffness + upper)
    row_index = jnp.arange(NI)[None, None, :]
    ones_like = jnp.ones((1, 1, NI), jnp.float32)
    chosen = jnp.where(row_index >= NI - shared_sizes[:, :, 1:2], up_weight[..., None], ones_like)
    chosen = jnp.where(row_index < shared_sizes[:, :, 0:1], low_weight[..., None], chosen)
    return chosen[..., None]


def batched_dot(matrices, vectors):
    def one_pair(pair):
        return jnp.dot(pair[0], pair[1], preferred_element_type=jnp.float32)
    return lax.map(one_pair, (matrices, vectors))


def reference(shared_sizes, stiffness, load_cases, schur_blocks, neumann_inverse, coarse_basis, coarse_dofs, coarse_inverse):
    groups, subs = stiffness.shape
    count = groups * subs
    cases = load_cases.shape[-1]
    order = coarse_inverse.shape[0]
    weight = interface_weights(shared_sizes, stiffness)
    schur_flat = schur_blocks.reshape(count, NI, NI)
    neumann_flat = neumann_inverse.reshape(count, NI, NI)
    basis32 = coarse_basis.astype(jnp.float32)
    dof_flat = coarse_dofs.reshape(-1).astype(jnp.int32)

    def operator_residual(solution):
        product = batched_dot(schur_flat, solution.astype(jnp.bfloat16).reshape(count, NI, cases))
        return load_cases - product.reshape(groups, subs, NI, cases)

    solution = jnp.zeros((groups, subs, NI, cases), jnp.float32)
    for sweep in range(ITERS):
        local = operator_residual(solution)
        weighted = (weight * assemble(local, shared_sizes)).astype(jnp.bfloat16)
        terms = jnp.einsum('gsji,gsib->gsjb', basis32, weighted.astype(jnp.float32))
        gathered = jnp.zeros((order, cases), jnp.float32).at[dof_flat].add(terms.reshape(-1, cases))
        solved = jnp.dot(coarse_inverse, gathered, precision=lax.Precision.HIGHEST)
        picked = solved[coarse_dofs].astype(jnp.bfloat16)
        correction = batched_dot(neumann_flat, weighted.reshape(count, NI, cases)).reshape(groups, subs, NI, cases)
        correction = correction + jnp.einsum('gsji,gsjb->gsib', basis32, picked.astype(jnp.float32))
        solution = solution + OMEGA * assemble(weight * correction, shared_sizes)
    residual = assemble(operator_residual(solution), shared_sizes)
    return solution, residual
```

```python
import functools
import math

import jax
import jax.numpy as jnp
from jax import lax
from jax.experimental import pallas as pl
from jax.experimental.pallas import tpu as pltpu
from jax.sharding import PartitionSpec as P

ITERS = 4
OMEGA = 0.6
SH = 256
COLS = 128
CORES = 2
STIFF_LANE = 64
F32 = jnp.float32
BF16 = jnp.bfloat16
BY_ROWS = (((1,), (1,)), ((), ()))


def iota(shape, dim):
    return lax.broadcasted_iota(jnp.int32, shape, dim)


def kernel(
    nx, nz, ny, chunks,
    share, info, loads_hbm, schur_hbm, neumann_hbm, basis_hbm, coarse_hbm,
    sol_hbm, res_hbm,
    schur, neumann, basis, coarse, halves,
    loads, local, field, sol, weighted, rounded,
    from_lower, from_upper, corr_lower, corr_upper,
    weight_head, weight_tail, perm,
    edge_out, edge_in, extended, extended_t,
    pick_rows, select, chosen, columns, columns_hl, coarse_k,
    terms, part_y, got_y, part_z, got_z, picked, picked_near,
    loc_sem, out_sem,
    h1s, h1r, h2s, h2r, nps, npr, xs, xr, cs, cr, ys, yr, zs, zr,
    gzs, gzr, gxs, gxr, gcs, gcr, bs, br,
):
    half = nz // CORES
    subs = nx * nz
    unknowns = loads.shape[1]
    ncl = basis.shape[0]
    order = coarse.shape[1]
    own_rows = coarse.shape[0]
    tail0 = unknowns - SH
    tiles = unknowns // SH
    edges = (0, tiles - 1)
    inner = tuple(range(1, tiles - 1))

    g, s = lax.axis_index("group"), lax.axis_index("sub")
    y, c = g // CORES, g % CORES
    z, x = s // nx, s % nx
    upper = (g, lax.rem(s + 1, subs))
    lower = (g, lax.rem(s + subs - 1, subs))
    x_peers = [(g, z * nx + lax.rem(x + d, nx)) for d in range(1, nx)]
    z_peers = [(g, lax.rem(z + d, nz) * nx + x) for d in range(1, nz)]
    y_peers = [(lax.rem(y + d, ny) * CORES + c, s) for d in range(1, ny)]
    core_peer = (y * CORES + 1 - c, s)

    share_low, share_up = share[0], share[1]

    def remote(src, dst, send, recv, to):
        return pltpu.make_async_remote_copy(
            src_ref=src, dst_ref=dst, send_sem=send, recv_sem=recv,
            device_id=to, device_id_type=pl.DeviceIdType.MESH,
        )

    def start(copies):
        for copy in copies:
            copy.start()

    def landed(copies):
        for copy in copies:
            copy.wait_recv()

    def sent(copies):
        for copy in copies:
            copy.wait_send()

    def rows(tile):
        return pl.ds(tile * SH, SH)

    def halo_local(ch):
        return (
            remote(local.at[ch, pl.ds(tail0, SH)], from_lower.at[ch], h1s.at[ch, 0], h1r.at[ch, 0], upper),
            remote(local.at[ch, pl.ds(0, SH)], from_upper.at[ch], h1s.at[ch, 1], h1r.at[ch, 1], lower),
        )

    def halo_field(ch):
        return (
            remote(field.at[ch, pl.ds(tail0, SH)], corr_lower.at[ch], h2s.at[ch, 0], h2r.at[ch, 0], upper),
            remote(field.at[ch, pl.ds(0, SH)], corr_upper.at[ch], h2s.at[ch, 1], h2r.at[ch, 1], lower),
        )

    def terms_x(k, ch):
        own = terms.at[k, ch, c, x]
        return [remote(own, own, xs.at[ch, d], xr.at[k, ch, d], to) for d, to in enumerate(x_peers)]

    def terms_core(k, ch):
        own = terms.at[k, ch, c]
        return (remote(own, own, cs.at[ch], cr.at[k, ch], core_peer),)

    def parts_y(k, ch):
        return [
            remote(part_y.at[ch, lax.rem(y + d + 1, ny)], got_y.at[k, ch, d], ys.at[ch, d], yr.at[k, ch, d], to)
            for d, to in enumerate(y_peers)
        ]

    def parts_z(k, ch):
        return [
            remote(part_z.at[ch, lax.rem(z + d + 1, nz)], got_z.at[k, ch, d], zs.at[ch, d], zr.at[k, ch, d], to)
            for d, to in enumerate(z_peers)
        ]

    def picked_halo(ch):
        return (
            remote(picked.at[ch], picked_near.at[ch, 0], nps.at[ch, 0], npr.at[ch, 0], upper),
            remote(picked.at[ch], picked_near.at[ch, 1], nps.at[ch, 1], npr.at[ch, 1], lower),
        )

    def basis_halo():
        return (
            remote(edge_out.at[0], edge_in.at[0], bs.at[0], br.at[0], upper),
            remote(edge_out.at[1], edge_in.at[1], bs.at[1], br.at[1], lower),
        )

    def columns_z():
        return [
            remote(chosen.at[lax.rem(z + d + 1, nz)], columns.at[c, x, lax.rem(z, half)], gzs.at[d], gzr.at[d], to)
            for d, to in enumerate(z_peers)
        ]

    def columns_x():
        own = columns.at[c, x]
        return [remote(own, own, gxs.at[d], gxr.at[d], to) for d, to in enumerate(x_peers)]

    def columns_core():
        own = columns.at[c]
        return (remote(own, own, gcs.at[0], gcr.at[0], core_peer),)

    load_in = [
        pltpu.make_async_copy(loads_hbm.at[:, pl.ds(ch * COLS, COLS)], loads.at[ch], loc_sem.at[ch])
        for ch in range(chunks)
    ]
    others = [
        pltpu.make_async_copy(src, dst, loc_sem.at[chunks + i])
        for i, (src, dst) in enumerate(
            ((basis_hbm, basis), (coarse_hbm, coarse), (neumann_hbm, neumann), (schur_hbm, schur))
        )
    ]
    start(load_in)
    start(others)
    barrier = pltpu.get_barrier_semaphore()
    peers = [upper, lower, *x_peers, *z_peers, *y_peers, core_peer]
    for peer in peers:
        pl.semaphore_signal(barrier, inc=1, device_id=peer, device_id_type=pl.DeviceIdType.MESH)
    pl.semaphore_wait(barrier, len(peers))

    turn = lax.rem(share_up, SH)
    turn_back = lax.rem(2 * SH - share_up, SH)
    for ch in range(chunks):
        load_in[ch].wait()
        loads[ch, tail0:, :] = pltpu.roll(loads[ch, tail0:, :], turn, axis=0)
        local[ch, :, :] = loads[ch, :, :]
        start(halo_local(ch))

    def stiffness_of(sub):
        row = info[pl.ds(g * subs + sub, 1), :]
        lane = iota((1, COLS), 1)
        return jnp.sum(jnp.where(lane == STIFF_LANE, row, 0.0), axis=1, keepdims=True)

    own_stiff = stiffness_of(s)
    low_stiff = stiffness_of(lower[1])
    up_stiff = stiffness_of(upper[1])
    w_low = own_stiff / (own_stiff + low_stiff)
    w_up = own_stiff / (own_stiff + up_stiff)
    n_low = low_stiff / (low_stiff + own_stiff)
    n_up = up_stiff / (up_stiff + own_stiff)
    in_low = iota((SH, COLS), 0) < share_low
    in_up = iota((SH, COLS), 0) < share_up
    weight_head[...] = jnp.where(in_low, w_low, 1.0)
    weight_tail[...] = jnp.where(in_up, w_up, 1.0)

    moved = (iota((SH, SH), 0) + (SH - share_up)) & (SH - 1)
    perm[...] = jnp.where(iota((SH, SH), 1) == moved, 1.0, 0.0).astype(BF16)
    others[0].wait()
    basis_tail = lax.dot_general(basis[:, tail0:], perm[...], BY_ROWS, preferred_element_type=F32)
    basis[:, tail0:] = basis_tail.astype(BF16)
    edge_out[0] = basis_tail
    edge_out[1] = basis[:, :SH].astype(F32)
    start(basis_halo())
    lane_low = iota((ncl, SH), 1) < share_low
    lane_up = iota((ncl, SH), 1) < share_up
    extended[...] = jnp.zeros_like(extended)
    extended[0:ncl, :] = basis[...].astype(F32)
    extended[0:ncl, :SH] = jnp.where(lane_low, w_low, 1.0) * extended[0:ncl, :SH]
    extended[0:ncl, tail0:] = jnp.where(lane_up, w_up, 1.0) * extended[0:ncl, tail0:]

    def dof_column(device):
        row = jnp.broadcast_to(info[pl.ds(device, 1), :], (ncl, COLS))
        hit = iota((ncl, COLS), 0) == iota((ncl, COLS), 1)
        return jnp.sum(jnp.where(hit, row, 0.0), axis=1, keepdims=True).astype(jnp.int32)

    others[1].wait()
    high = coarse[...].astype(BF16)
    halves[0:own_rows, :] = high
    halves[own_rows:, :] = (coarse[...] - high.astype(F32)).astype(BF16)

    def choose(zt, carry):
        for cc in range(CORES):
            for xx in range(nx):
                column = dof_column((y * CORES + cc) * subs + zt * nx + xx)
                at = (cc * nx + xx) * ncl
                select[at : at + ncl, :] = jnp.where(iota((ncl, order), 1) == column, 1.0, 0.0).astype(BF16)
        both = lax.dot_general(select[...], halves[...], BY_ROWS, preferred_element_type=F32)
        chosen[zt] = both[:, :own_rows] + both[:, own_rows:]
        return carry

    lax.fori_loop(0, nz, choose, 0)

    sends_here = z // half == c

    @pl.when(sends_here)
    def _():
        start(columns_z())
        columns[c, x, lax.rem(z, half)] = chosen[z]

    for yy in range(ny):
        for zz in range(nz):
            column = jnp.broadcast_to(dof_column((yy * CORES + c) * subs + zz * nx + x), (ncl, order))
            at = (yy * nz + zz) * ncl
            pick_rows[at : at + ncl, :] = jnp.where(iota((ncl, order), 1) == column, 1.0, 0.0).astype(BF16)

    def align(matrix):
        wide = jnp.dot(perm[...], matrix[tail0:, :], preferred_element_type=F32)
        matrix[tail0:, :] = wide.astype(BF16)

        def turn_columns(tile, carry):
            at = pl.ds(pl.multiple_of(tile * SH, SH), SH)
            swapped = lax.dot_general(matrix[at, tail0:], perm[...], BY_ROWS, preferred_element_type=F32)
            matrix[at, tail0:] = swapped.astype(BF16)
            return carry

        lax.fori_loop(0, tiles, turn_columns, 0)

    others[2].wait()
    align(neumann)

    for d, copy in enumerate(columns_z()):
        sender = lax.rem(z + nz - 1 - d, nz)
        pl.when(sender // half == c)(copy.wait_recv)
    start(columns_x())

    others[3].wait()
    align(schur)

    @pl.when(sends_here)
    def _():
        sent(columns_z())

    sol[...] = jnp.zeros_like(sol)

    def each_chunk(step):
        def body(ch, carry):
            step(ch)
            return carry

        lax.fori_loop(0, chunks, body, 0)

    def weigh(k, ch):
        landed(halo_local(ch))
        head = local[ch, :SH, :] + jnp.where(in_low, from_lower[ch], 0.0)
        weighted[ch, :SH, :] = (weight_head[...] * head).astype(BF16)
        weighted[ch, SH:tail0, :] = local[ch, SH:tail0, :].astype(BF16)
        tail = local[ch, tail0:, :] + jnp.where(in_up, from_upper[ch], 0.0)
        weighted[ch, tail0:, :] = (weight_tail[...] * tail).astype(BF16)
        terms[k, ch, c, x] = jnp.dot(basis[...], weighted[ch], preferred_element_type=F32)
        start(terms_x(k, ch))
        for tile in edges + inner:
            product = jnp.dot(neumann[rows(tile), :], weighted[ch], preferred_element_type=F32)
            if tile == 0:
                product = weight_head[...] * product
            if tile == tiles - 1:
                product = weight_tail[...] * product
            field[ch, rows(tile), :] = product
            if tile == edges[-1]:
                start(halo_field(ch))

    def to_core(k, ch):
        landed(terms_x(k, ch))
        start(terms_core(k, ch))

    def solve(k, ch):
        landed(terms_core(k, ch))
        mine = terms[k, ch].reshape(CORES * nx * ncl, COLS)
        high = mine.astype(BF16)
        low = (mine - high.astype(F32)).astype(BF16)
        stacked = jnp.concatenate([high, high, low], axis=0)
        solved = jnp.dot(coarse_k[...], stacked, preferred_element_type=F32)
        part_y[ch] = solved.reshape(ny, nz * ncl, COLS)
        start(parts_y(k, ch))

    def sum_y(k, ch):
        copies = parts_y(k, ch)
        landed(copies)
        total = part_y[ch, y]
        for d in range(ny - 1):
            total = total + got_y[k, ch, d]
        part_z[ch] = total.reshape(nz, ncl, COLS)
        start(parts_z(k, ch))
        sent(copies)

    def sum_z(k, ch):
        copies = parts_z(k, ch)
        landed(copies)
        total = part_z[ch, z]
        for d in range(nz - 1):
            total = total + got_z[k, ch, d]
        picked[ch] = total
        start(picked_halo(ch))
        sent(copies)

    def advance(k, ch):
        near = picked_halo(ch)
        landed(near)
        halo = halo_field(ch)
        landed(halo)
        stacked = jnp.concatenate(
            [picked[ch], picked_near[ch, 0], picked_near[ch, 1], jnp.zeros((COLS - 3 * ncl, COLS), F32)], axis=0
        ).astype(BF16)
        sent(near)
        sent(halo)
        for tile in range(tiles):
            change = field[ch, rows(tile), :] + jnp.dot(
                extended_t[rows(tile), :], stacked, preferred_element_type=F32
            )
            if tile == 0:
                change = change + jnp.where(in_low, corr_lower[ch], 0.0)
            if tile == tiles - 1:
                change = change + jnp.where(in_up, corr_upper[ch], 0.0)
            new = sol[ch, rows(tile), :] + OMEGA * change
            sol[ch, rows(tile), :] = new
            rounded[rows(tile), :] = new.astype(BF16)
        out = halo_local(ch)
        sent(out)
        for tile in edges + inner:
            product = jnp.dot(schur[rows(tile), :], rounded[...], preferred_element_type=F32)
            local[ch, rows(tile), :] = loads[ch, rows(tile), :] - product
            if tile == edges[-1]:
                start(out)
        sent(terms_x(k, ch))
        sent(terms_core(k, ch))

    def finish_setup():
        copies = columns_x()
        landed(copies)
        start(columns_core())
        sent(copies)
        edge = basis_halo()
        landed(edge)
        extended[ncl : 2 * ncl, :SH] = jnp.where(lane_low, n_low * edge_in[0], 0.0)
        extended[2 * ncl : 3 * ncl, tail0:] = jnp.where(lane_up, n_up * edge_in[1], 0.0)
        extended_t[...] = extended[...].T.astype(BF16)
        sent(edge)
        landed(columns_core())
        wide = CORES * nx * ncl
        for cc in range(CORES):
            for xx in range(nx):
                for i in range(half):
                    block = columns[cc, xx, i]
                    high = block.astype(BF16)
                    at = ((cc * half + i) * nx + xx) * own_rows
                    columns_hl[:wide, at : at + own_rows] = high
                    columns_hl[wide:, at : at + own_rows] = (block - high.astype(F32)).astype(BF16)

        def row_tile(tile, carry):
            at = pl.ds(pl.multiple_of(tile * COLS, COLS), COLS)
            both = lax.dot_general(pick_rows[at, :], columns_hl[...], BY_ROWS, preferred_element_type=F32)
            high = both[:, :wide].astype(BF16)
            coarse_k[at, :wide] = high
            coarse_k[at, wide : 2 * wide] = both[:, wide:].astype(BF16)
            coarse_k[at, 2 * wide :] = high
            return carry

        lax.fori_loop(0, pick_rows.shape[0] // COLS, row_tile, 0)
        sent(columns_core())

    def iteration(k, carry):
        each_chunk(functools.partial(weigh, k))
        each_chunk(functools.partial(to_core, k))
        pl.when(k == 0)(finish_setup)
        each_chunk(functools.partial(solve, k))
        each_chunk(functools.partial(sum_y, k))
        each_chunk(functools.partial(sum_z, k))
        each_chunk(functools.partial(advance, k))
        return carry

    lax.fori_loop(0, ITERS, iteration, 0)

    out_copies = []
    for ch in range(chunks):
        sol[ch, tail0:, :] = pltpu.roll(sol[ch, tail0:, :], turn_back, axis=0)
        copy = pltpu.make_async_copy(sol.at[ch], sol_hbm.at[:, pl.ds(ch * COLS, COLS)], out_sem.at[ch])
        copy.start()
        out_copies.append(copy)
    for ch in range(chunks):
        copies = halo_local(ch)
        landed(copies)
        field[ch, :SH, :] = local[ch, :SH, :] + jnp.where(in_low, from_lower[ch], 0.0)
        field[ch, SH:tail0, :] = local[ch, SH:tail0, :]
        tail = local[ch, tail0:, :] + jnp.where(in_up, from_upper[ch], 0.0)
        field[ch, tail0:, :] = pltpu.roll(tail, turn_back, axis=0)
        copy = pltpu.make_async_copy(field.at[ch], res_hbm.at[:, pl.ds(ch * COLS, COLS)], out_sem.at[chunks + ch])
        copy.start()
        out_copies.append(copy)
        sent(copies)
    for copy in out_copies:
        copy.wait()


def on_device(
    shared_sizes,
    stiffness,
    load_cases,
    schur_blocks,
    neumann_inverse,
    coarse_basis,
    coarse_dofs,
    coarse_inverse,
):
    groups, subs = lax.axis_size("group"), lax.axis_size("sub")
    nx = math.isqrt(subs)
    nz, ny = subs // nx, groups // CORES
    half = nz // CORES
    unknowns, cases = load_cases.shape[2:]
    chunks = cases // COLS
    ncl = coarse_basis.shape[2]
    own_rows, order = coarse_inverse.shape
    wide, tall = CORES * nx * ncl, ny * nz * ncl

    mine = jnp.zeros((1, COLS), F32)
    mine = mine.at[:, :ncl].set(coarse_dofs[0].astype(F32))
    mine = mine.at[:, STIFF_LANE].set(stiffness[0])
    info = lax.all_gather(mine, ("group", "sub"), axis=0, tiled=True)

    dma = pltpu.SemaphoreType.DMA
    vmem = pltpu.VMEM
    scratch = [
        vmem((unknowns, unknowns), BF16),
        vmem((unknowns, unknowns), BF16),
        vmem((ncl, unknowns), BF16),
        vmem((own_rows, order), F32),
        vmem((2 * own_rows, order), BF16),
        vmem((chunks, unknowns, COLS), F32),
        vmem((chunks, unknowns, COLS), F32),
        vmem((chunks, unknowns, COLS), F32),
        vmem((chunks, unknowns, COLS), F32),
        vmem((chunks, unknowns, COLS), BF16),
        vmem((unknowns, COLS), BF16),
        vmem((chunks, SH, COLS), F32),
        vmem((chunks, SH, COLS), F32),
        vmem((chunks, SH, COLS), F32),
        vmem((chunks, SH, COLS), F32),
        vmem((SH, COLS), F32),
        vmem((SH, COLS), F32),
        vmem((SH, SH), BF16),
        vmem((2, ncl, SH), F32),
        vmem((2, ncl, SH), F32),
        vmem((COLS, unknowns), F32),
        vmem((unknowns, COLS), BF16),
        vmem((tall, order), BF16),
        vmem((wide, order), BF16),
        vmem((nz, wide, own_rows), F32),
        vmem((CORES, nx, half, wide, own_rows), F32),
        vmem((2 * wide, order), BF16),
        vmem((tall, 3 * wide), BF16),
        vmem((ITERS, chunks, CORES, nx, ncl, COLS), F32),
        vmem((chunks, ny, nz * ncl, COLS), F32),
        vmem((ITERS, chunks, ny - 1, nz * ncl, COLS), F32),
        vmem((chunks, nz, ncl, COLS), F32),
        vmem((ITERS, chunks, nz - 1, ncl, COLS), F32),
        vmem((chunks, ncl, COLS), F32),
        vmem((chunks, 2, ncl, COLS), F32),
        dma((chunks + 4,)),
        dma((2 * chunks,)),
        dma((chunks, 2)), dma((chunks, 2)),
        dma((chunks, 2)), dma((chunks, 2)),
        dma((chunks, 2)), dma((chunks, 2)),
        dma((chunks, nx - 1)), dma((ITERS, chunks, nx - 1)),
        dma((chunks,)), dma((ITERS, chunks)),
        dma((chunks, ny - 1)), dma((ITERS, chunks, ny - 1)),
        dma((chunks, nz - 1)), dma((ITERS, chunks, nz - 1)),
        dma((nz - 1,)), dma((nz - 1,)),
        dma((nx - 1,)), dma((nx - 1,)),
        dma((1,)), dma((1,)),
        dma((2,)), dma((2,)),
    ]
    anywhere = pl.BlockSpec(memory_space=pl.ANY)
    out = jax.ShapeDtypeStruct((unknowns, cases), F32)
    sol, res = pl.pallas_call(
        functools.partial(kernel, nx, nz, ny, chunks),
        out_shape=(out, out),
        in_specs=[pl.BlockSpec(memory_space=pltpu.SMEM), pl.BlockSpec(memory_space=pltpu.VMEM)] + [anywhere] * 5,
        out_specs=(anywhere, anywhere),
        scratch_shapes=scratch,
        compiler_params=pltpu.CompilerParams(
            collective_id=0, has_side_effects=True, vmem_limit_bytes=56 * 1024 * 1024
        ),
        cost_estimate=pl.CostEstimate(flops=2 * 9 * unknowns * unknowns * cases, bytes_accessed=1 << 24, transcendentals=0),
    )(
        shared_sizes[0, 0],
        info,
        load_cases[0, 0],
        schur_blocks[0, 0],
        neumann_inverse[0, 0],
        coarse_basis[0, 0],
        coarse_inverse,
    )
    return (sol[None, None], res[None, None])


def solution(mesh):
    return jax.shard_map(
        on_device,
        mesh=mesh,
        in_specs=(
            P("group", "sub", None),
            P("group", "sub"),
            P("group", "sub", None, None),
            P("group", "sub", None, None),
            P("group", "sub", None, None),
            P("group", "sub", None, None),
            P("group", "sub", None),
            P("sub", None),
        ),
        out_specs=(P("group", "sub", None, None), P("group", "sub", None, None)),
        check_vma=False,
    )
```

```python
import functools
import math

import jax
import jax.numpy as jnp
from jax import lax
from jax.experimental import pallas as pl
from jax.experimental.pallas import tpu as pltpu
from jax.sharding import PartitionSpec as P

ITERS = 4
OMEGA = 0.6
SH = 256
COLS = 128
CORES = 2
F32 = jnp.float32
BF16 = jnp.bfloat16


def iota(shape, dim):
    return lax.broadcasted_iota(jnp.int32, shape, dim)


def kernel(
    nx, nz, ny, chunks,
    share, stiff, dofs, loads_hbm, schur_hbm, neumann_hbm, basis_hbm, coarse_hbm,
    sol_hbm, res_hbm,
    schur, neumann, basis, coarse, halves,
    loads, local, field, sol, weighted, rounded,
    from_lower, from_upper, corr_lower, corr_upper,
    weight_head, weight_tail, perm, perm_t,
    edge_out, edge_in, extended, extended_t,
    pick_rows, select, chosen, columns, columns_hl, coarse_k,
    terms, part_y, got_y, part_z, got_z, near_z,
    facts, facts_near, facts_far, facts_side,
    loc_sem, out_sem,
    h1s, h1r, h2s, h2r, nps, npr, xs, xr, cs, cr, ys, yr, zs, zr,
    gzs, gzr, gxs, gxr, gcs, gcr, bs, br,
    fxs, fxr, fcs, fcr, fzs, fzr, fbs, fbr, fys, fyr, fns, fnr,
):
    half = nz // CORES
    subs = nx * nz
    unknowns = loads.shape[1]
    ncl = basis.shape[0]
    order = coarse.shape[1]
    own_rows = coarse.shape[0]
    tail0 = unknowns - SH
    tiles = unknowns // SH
    edges = (0, tiles - 1)
    inner = tuple(range(1, tiles - 1))

    g, s = lax.axis_index("group"), lax.axis_index("sub")
    y, c = g // CORES, g % CORES
    z, x = s // nx, s % nx
    upper = (g, lax.rem(s + 1, subs))
    lower = (g, lax.rem(s + subs - 1, subs))
    x_peers = [(g, z * nx + lax.rem(x + d, nx)) for d in range(1, nx)]
    z_peers = [(g, lax.rem(z + d, nz) * nx + x) for d in range(1, nz)]
    in_column = [lax.rem(z + d, nz) * nx + x for d in range(nz)]
    beside = [[(g, lax.rem(sub + step, subs)) for sub in in_column] for step in (1, subs - 1)]
    y_peers = [(lax.rem(y + d, ny) * CORES + c, s) for d in range(1, ny)]
    core_peer = (y * CORES + 1 - c, s)

    share_low, share_up = share[0], share[1]

    def remote(src, dst, send, recv, to):
        return pltpu.make_async_remote_copy(
            src_ref=src, dst_ref=dst, send_sem=send, recv_sem=recv,
            device_id=to, device_id_type=pl.DeviceIdType.MESH,
        )

    def start(copies):
        for copy in copies:
            copy.start()

    def landed(copies):
        for copy in copies:
            copy.wait_recv()

    def sent(copies):
        for copy in copies:
            copy.wait_send()

    def rows(tile):
        return pl.ds(tile * SH, SH)

    def halo_local(ch):
        return (
            remote(local.at[ch, pl.ds(tail0, SH)], from_lower.at[ch], h1s.at[ch, 0], h1r.at[ch, 0], upper),
            remote(local.at[ch, pl.ds(0, SH)], from_upper.at[ch], h1s.at[ch, 1], h1r.at[ch, 1], lower),
        )

    def halo_field(ch):
        return (
            remote(field.at[ch, pl.ds(tail0, SH)], corr_lower.at[ch], h2s.at[ch, 0], h2r.at[ch, 0], upper),
            remote(field.at[ch, pl.ds(0, SH)], corr_upper.at[ch], h2s.at[ch, 1], h2r.at[ch, 1], lower),
        )

    def terms_x(k, ch):
        own = terms.at[k, ch, c, x]
        return [remote(own, own, xs.at[ch, d], xr.at[k, ch, d], to) for d, to in enumerate(x_peers)]

    def terms_core(k, ch):
        own = terms.at[k, ch, c]
        return (remote(own, own, cs.at[ch], cr.at[k, ch], core_peer),)

    def parts_y(k, ch):
        return [
            remote(part_y.at[ch, lax.rem(y + d + 1, ny)], got_y.at[k, ch, d], ys.at[ch, d], yr.at[k, ch, d], to)
            for d, to in enumerate(y_peers)
        ]

    def parts_z(k, ch):
        return [
            remote(part_z.at[ch, lax.rem(z + d + 1, nz)], got_z.at[k, ch, z], zs.at[ch, d], zr.at[k, ch, d], to)
            for d, to in enumerate(z_peers)
        ]

    def parts_beside(k, ch):
        return [
            remote(
                part_z.at[ch, lax.rem(z + d, nz)], near_z.at[k, ch, side, z],
                nps.at[ch, side, d], npr.at[k, ch, side, d], beside[side][d],
            )
            for side in range(2)
            for d in range(nz)
        ]

    def basis_halo():
        return (
            remote(edge_out.at[0], edge_in.at[0], bs.at[0], br.at[0], upper),
            remote(edge_out.at[1], edge_in.at[1], bs.at[1], br.at[1], lower),
        )

    def columns_z():
        return [
            remote(chosen.at[lax.rem(z + d + 1, nz)], columns.at[c, x, lax.rem(z, half)], gzs.at[d], gzr.at[d], to)
            for d, to in enumerate(z_peers)
        ]

    def columns_x():
        own = columns.at[c, x]
        return [remote(own, own, gxs.at[d], gxr.at[d], to) for d, to in enumerate(x_peers)]

    def columns_core():
        own = columns.at[c]
        return (remote(own, own, gcs.at[0], gcr.at[0], core_peer),)

    def facts_x():
        own = facts_near.at[z, c, x]
        return [remote(facts, own, fxs.at[d], fxr.at[d], to) for d, to in enumerate(x_peers)]

    def facts_core():
        own = facts_near.at[z, c]
        return (remote(own, own, fcs.at[0], fcr.at[0], core_peer),)

    def facts_z():
        own = facts_near.at[z]
        return [remote(own, own, fzs.at[d], fzr.at[d], to) for d, to in enumerate(z_peers)]

    def far_z():
        return [remote(facts, facts_far.at[y, z], fbs.at[d], fbr.at[d], to) for d, to in enumerate(z_peers)]

    def far_y():
        own = facts_far.at[y]
        return [remote(own, own, fys.at[d], fyr.at[d], to) for d, to in enumerate(y_peers)]

    def facts_beside():
        return (
            remote(facts, facts_side.at[0], fns.at[0], fnr.at[0], upper),
            remote(facts, facts_side.at[1], fns.at[1], fnr.at[1], lower),
        )

    load_in = [
        pltpu.make_async_copy(loads_hbm.at[:, pl.ds(ch * COLS, COLS)], loads.at[ch], loc_sem.at[ch])
        for ch in range(chunks)
    ]
    others = [
        pltpu.make_async_copy(src, dst, loc_sem.at[chunks + i])
        for i, (src, dst) in enumerate(
            ((basis_hbm, basis), (coarse_hbm, coarse), (neumann_hbm, neumann), (schur_hbm, schur))
        )
    ]
    start(load_in)
    start(others)
    facts[...] = jnp.full(facts.shape, stiff[0], F32)
    facts[0:1, :ncl] = dofs[...].astype(F32)
    facts_near[z, c, x] = facts[...]
    facts_far[y, z] = facts[...]
    barrier = pltpu.get_barrier_semaphore()
    peers = [*beside[0], *beside[1], *x_peers, *z_peers, *y_peers, core_peer]
    for peer in peers:
        pl.semaphore_signal(barrier, inc=1, device_id=peer, device_id_type=pl.DeviceIdType.MESH)
    pl.semaphore_wait(barrier, len(peers))

    start(facts_beside())
    start(facts_x())
    start(far_z())

    turn = lax.rem(share_up, SH)
    turn_back = lax.rem(2 * SH - share_up, SH)
    for ch in range(chunks):
        load_in[ch].wait()
        loads[ch, tail0:, :] = pltpu.roll(loads[ch, tail0:, :], turn, axis=0)
        local[ch, :, :] = loads[ch, :, :]
        start(halo_local(ch))

    landed(facts_x())
    start(facts_core())
    landed(far_z())
    start(far_y())
    landed(facts_beside())
    own_stiff = facts[1:2, 0:1]
    low_stiff = facts_side[0, 1:2, 0:1]
    up_stiff = facts_side[1, 1:2, 0:1]
    w_low = own_stiff / (own_stiff + low_stiff)
    w_up = own_stiff / (own_stiff + up_stiff)
    n_low = low_stiff / (low_stiff + own_stiff)
    n_up = up_stiff / (up_stiff + own_stiff)
    in_low = iota((SH, COLS), 0) < share_low
    in_up = iota((SH, COLS), 0) < share_up
    weight_head[...] = jnp.where(in_low, w_low, 1.0)
    weight_tail[...] = jnp.where(in_up, w_up, 1.0)

    moved = (iota((SH, SH), 0) + (SH - share_up)) & (SH - 1)
    perm[...] = jnp.where(iota((SH, SH), 1) == moved, 1.0, 0.0).astype(BF16)
    moved_lane = (iota((SH, SH), 1) + (SH - share_up)) & (SH - 1)
    perm_t[...] = jnp.where(iota((SH, SH), 0) == moved_lane, 1.0, 0.0).astype(BF16)
    others[0].wait()
    basis_tail = jnp.dot(basis[:, tail0:], perm_t[...], preferred_element_type=F32)
    basis[:, tail0:] = basis_tail.astype(BF16)
    edge_out[0] = basis_tail
    edge_out[1] = basis[:, :SH].astype(F32)
    start(basis_halo())
    lane_low = iota((ncl, SH), 1) < share_low
    lane_up = iota((ncl, SH), 1) < share_up
    extended[...] = jnp.zeros_like(extended)
    extended[0:ncl, :] = basis[...].astype(F32)
    extended[0:ncl, :SH] = jnp.where(lane_low, w_low, 1.0) * extended[0:ncl, :SH]
    extended[0:ncl, tail0:] = jnp.where(lane_up, w_up, 1.0) * extended[0:ncl, tail0:]

    def dof_column(row):
        row = jnp.broadcast_to(row, (ncl, COLS))
        hit = iota((ncl, COLS), 0) == iota((ncl, COLS), 1)
        return jnp.sum(jnp.where(hit, row, 0.0), axis=1, keepdims=True).astype(jnp.int32)

    landed(facts_core())
    start(facts_z())
    others[1].wait()
    high = coarse[...].astype(BF16)
    halves[0:own_rows, :] = high
    halves[own_rows:, :] = (coarse[...] - high.astype(F32)).astype(BF16)
    landed(facts_z())

    def choose(zt, carry):
        row = jnp.concatenate(
            [facts_near[zt, cc, xx, 0:1, :ncl] for cc in range(CORES) for xx in range(nx)], axis=1
        ).astype(jnp.int32)

        def hot(part, carry):
            at = pl.ds(pl.multiple_of(part * SH, SH), SH)
            index = iota((SH, row.shape[1]), 0) + part * SH
            select[at, :] = jnp.where(index == row, 1.0, 0.0).astype(BF16)
            return carry

        lax.fori_loop(0, order // SH, hot, 0)
        both = jnp.dot(halves[...], select[...], preferred_element_type=F32)
        chosen[zt] = both[:own_rows] + both[own_rows:]
        return carry

    lax.fori_loop(0, nz, choose, 0)

    sends_here = z // half == c

    @pl.when(sends_here)
    def _():
        start(columns_z())
        columns[c, x, lax.rem(z, half)] = chosen[z]

    edge = basis_halo()
    landed(edge)
    extended[ncl : 2 * ncl, :SH] = jnp.where(lane_low, n_low * edge_in[0], 0.0)
    extended[2 * ncl : 3 * ncl, tail0:] = jnp.where(lane_up, n_up * edge_in[1], 0.0)
    low = extended[...] - extended[...].astype(BF16).astype(F32)
    extended_t[:, :COLS] = extended[...].T.astype(BF16)
    extended_t[:, COLS:] = low.T.astype(BF16)
    sent(edge)
    landed(far_y())
    for yy in range(ny):
        for zz in range(nz):
            column = jnp.broadcast_to(dof_column(facts_far[yy, zz, 0:1, :]), (ncl, order))
            at = (yy * nz + zz) * ncl
            pick_rows[at : at + ncl, :] = jnp.where(iota((ncl, order), 1) == column, 1.0, 0.0).astype(BF16)

    def align(matrix):
        wide = jnp.dot(perm[...], matrix[tail0:, :], preferred_element_type=F32)
        matrix[tail0:, :] = wide.astype(BF16)

        def turn_columns(tile, carry):
            at = pl.ds(pl.multiple_of(tile * SH, SH), SH)
            swapped = jnp.dot(matrix[at, tail0:], perm_t[...], preferred_element_type=F32)
            matrix[at, tail0:] = swapped.astype(BF16)
            return carry

        lax.fori_loop(0, tiles, turn_columns, 0)

    others[2].wait()
    align(neumann)

    for d, copy in enumerate(columns_z()):
        sender = lax.rem(z + nz - 1 - d, nz)
        pl.when(sender // half == c)(copy.wait_recv)
    start(columns_x())

    others[3].wait()
    align(schur)

    @pl.when(sends_here)
    def _():
        sent(columns_z())

    sol[...] = jnp.zeros_like(sol)
    for copies in (facts_beside(), facts_x(), far_z(), facts_core(), far_y(), facts_z()):
        sent(copies)

    def weigh(k, ch):
        landed(halo_local(ch))
        head = local[ch, :SH, :] + jnp.where(in_low, from_lower[ch], 0.0)
        weighted[ch, :SH, :] = (weight_head[...] * head).astype(BF16)
        weighted[ch, SH:tail0, :] = local[ch, SH:tail0, :].astype(BF16)
        tail = local[ch, tail0:, :] + jnp.where(in_up, from_upper[ch], 0.0)
        weighted[ch, tail0:, :] = (weight_tail[...] * tail).astype(BF16)
        terms[k, ch, c, x] = jnp.dot(basis[...], weighted[ch], preferred_element_type=F32)
        start(terms_x(k, ch))
        for tile in edges + inner:
            product = jnp.dot(neumann[rows(tile), :], weighted[ch], preferred_element_type=F32)
            if tile == 0:
                product = weight_head[...] * product
            if tile == tiles - 1:
                product = weight_tail[...] * product
            field[ch, rows(tile), :] = product
            if tile == edges[-1]:
                start(halo_field(ch))

    def to_core(k, ch):
        landed(terms_x(k, ch))
        start(terms_core(k, ch))

    def solve(k, ch):
        landed(terms_core(k, ch))
        mine = terms[k, ch].reshape(CORES * nx * ncl, COLS)
        high = mine.astype(BF16)
        low = (mine - high.astype(F32)).astype(BF16)
        stacked = jnp.concatenate([high, high, low], axis=0)
        solved = jnp.dot(coarse_k[...], stacked, preferred_element_type=F32)
        part_y[ch] = solved.reshape(ny, nz * ncl, COLS)
        start(parts_y(k, ch))

    def sum_y(k, ch):
        copies = parts_y(k, ch)
        landed(copies)
        whole = part_y[ch, y]
        for d in range(ny - 1):
            whole = whole + got_y[k, ch, d]
        part_z[ch] = whole.reshape(nz, ncl, COLS)
        got_z[k, ch, z] = part_z[ch, z]
        start(parts_z(k, ch) + parts_beside(k, ch))
        sent(copies)

    def total(parts):
        result = parts[0]
        for i in range(1, nz):
            result = result + parts[i]
        return result

    def advance(k, ch):
        parts = parts_z(k, ch) + parts_beside(k, ch)
        landed(parts)
        halo = halo_field(ch)
        landed(halo)
        stacked = jnp.concatenate(
            [total(got_z.at[k, ch]), total(near_z.at[k, ch, 0]), total(near_z.at[k, ch, 1]), jnp.zeros((COLS - 3 * ncl, COLS), F32)], axis=0
        ).astype(BF16)
        stacked = jnp.concatenate([stacked, stacked], axis=0)
        sent(parts)
        sent(halo)
        for tile in range(tiles):
            change = field[ch, rows(tile), :] + jnp.dot(
                extended_t[rows(tile), :], stacked, preferred_element_type=F32
            )
            if tile == 0:
                change = change + jnp.where(in_low, corr_lower[ch], 0.0)
            if tile == tiles - 1:
                change = change + jnp.where(in_up, corr_upper[ch], 0.0)
            new = sol[ch, rows(tile), :] + OMEGA * change
            sol[ch, rows(tile), :] = new
            rounded[rows(tile), :] = new.astype(BF16)
        out = halo_local(ch)
        sent(out)
        for tile in edges + inner:
            product = jnp.dot(schur[rows(tile), :], rounded[...], preferred_element_type=F32)
            local[ch, rows(tile), :] = loads[ch, rows(tile), :] - product
            if tile == edges[-1]:
                start(out)
        sent(terms_x(k, ch))
        sent(terms_core(k, ch))

    def finish_setup():
        copies = columns_x()
        landed(copies)
        start(columns_core())
        sent(copies)
        landed(columns_core())
        wide = CORES * nx * ncl
        for cc in range(CORES):
            for xx in range(nx):
                for i in range(half):
                    block = columns[cc, xx, i]
                    high = block.astype(BF16)
                    at = ((cc * half + i) * nx + xx) * own_rows
                    columns_hl[at : at + own_rows, :wide] = high
                    columns_hl[at : at + own_rows, wide:] = (block - high.astype(F32)).astype(BF16)

        step = min(SH, pick_rows.shape[0])

        def row_tile(tile, carry):
            at = pl.ds(pl.multiple_of(tile * step, step), step)
            both = jnp.dot(pick_rows[at, :], columns_hl[...], preferred_element_type=F32)
            high = both[:, :wide].astype(BF16)
            coarse_k[at, :wide] = high
            coarse_k[at, wide : 2 * wide] = both[:, wide:].astype(BF16)
            coarse_k[at, 2 * wide :] = high
            return carry

        lax.fori_loop(0, pick_rows.shape[0] // step, row_tile, 0)
        sent(columns_core())

    def each_chunk(step):
        def body(ch, carry):
            step(0, ch)
            return carry

        lax.fori_loop(0, chunks, body, 0)

    lanes = chunks + 1

    def tick(now, carry):
        def run(step, late, first=0):
            turn = now - late

            @pl.when((turn >= first * lanes) & (turn < ITERS * lanes) & (lax.rem(turn + lanes, lanes) < chunks))
            def _():
                step(turn // lanes, lax.rem(turn, lanes))

        run(to_core, 1, 1)
        run(sum_y, 2)
        run(solve, 1)
        run(advance, 3)
        run(weigh, 0, 1)
        return carry

    each_chunk(weigh)
    each_chunk(to_core)
    finish_setup()
    lax.fori_loop(1, ITERS * lanes + 3 - 1, tick, 0)

    out_copies = []
    for ch in range(chunks):
        sol[ch, tail0:, :] = pltpu.roll(sol[ch, tail0:, :], turn_back, axis=0)
        copy = pltpu.make_async_copy(sol.at[ch], sol_hbm.at[:, pl.ds(ch * COLS, COLS)], out_sem.at[ch])
        copy.start()
        out_copies.append(copy)
    for ch in range(chunks):
        copies = halo_local(ch)
        landed(copies)
        field[ch, :SH, :] = local[ch, :SH, :] + jnp.where(in_low, from_lower[ch], 0.0)
        field[ch, SH:tail0, :] = local[ch, SH:tail0, :]
        tail = local[ch, tail0:, :] + jnp.where(in_up, from_upper[ch], 0.0)
        field[ch, tail0:, :] = pltpu.roll(tail, turn_back, axis=0)
        copy = pltpu.make_async_copy(field.at[ch], res_hbm.at[:, pl.ds(ch * COLS, COLS)], out_sem.at[chunks + ch])
        copy.start()
        out_copies.append(copy)
        sent(copies)
    for copy in out_copies:
        copy.wait()


def on_device(
    shared_sizes,
    stiffness,
    load_cases,
    schur_blocks,
    neumann_inverse,
    coarse_basis,
    coarse_dofs,
    coarse_inverse,
):
    groups, subs = lax.axis_size("group"), lax.axis_size("sub")
    nx = math.isqrt(subs)
    nz, ny = subs // nx, groups // CORES
    half = nz // CORES
    unknowns, cases = load_cases.shape[2:]
    chunks = cases // COLS
    ncl = coarse_basis.shape[2]
    own_rows, order = coarse_inverse.shape
    wide, tall = CORES * nx * ncl, ny * nz * ncl

    dma = pltpu.SemaphoreType.DMA
    vmem = pltpu.VMEM
    scratch = [
        vmem((unknowns, unknowns), BF16),
        vmem((unknowns, unknowns), BF16),
        vmem((ncl, unknowns), BF16),
        vmem((own_rows, order), F32),
        vmem((2 * own_rows, order), BF16),
        vmem((chunks, unknowns, COLS), F32),
        vmem((chunks, unknowns, COLS), F32),
        vmem((chunks, unknowns, COLS), F32),
        vmem((chunks, unknowns, COLS), F32),
        vmem((chunks, unknowns, COLS), BF16),
        vmem((unknowns, COLS), BF16),
        vmem((chunks, SH, COLS), F32),
        vmem((chunks, SH, COLS), F32),
        vmem((chunks, SH, COLS), F32),
        vmem((chunks, SH, COLS), F32),
        vmem((SH, COLS), F32),
        vmem((SH, COLS), F32),
        vmem((SH, SH), BF16),
        vmem((SH, SH), BF16),
        vmem((2, ncl, SH), F32),
        vmem((2, ncl, SH), F32),
        vmem((COLS, unknowns), F32),
        vmem((unknowns, 2 * COLS), BF16),
        vmem((tall, order), BF16),
        vmem((order, wide), BF16),
        vmem((nz, own_rows, wide), F32),
        vmem((CORES, nx, half, own_rows, wide), F32),
        vmem((order, 2 * wide), BF16),
        vmem((tall, 3 * wide), BF16),
        vmem((ITERS, chunks, CORES, nx, ncl, COLS), F32),
        vmem((chunks, ny, nz * ncl, COLS), F32),
        vmem((ITERS, chunks, ny - 1, nz * ncl, COLS), F32),
        vmem((chunks, nz, ncl, COLS), F32),
        vmem((ITERS, chunks, nz, ncl, COLS), F32),
        vmem((ITERS, chunks, 2, nz, ncl, COLS), F32),
        vmem((8, COLS), F32),
        vmem((nz, CORES, nx, 8, COLS), F32),
        vmem((ny, nz, 8, COLS), F32),
        vmem((2, 8, COLS), F32),
        dma((chunks + 4,)),
        dma((2 * chunks,)),
        dma((chunks, 2)), dma((chunks, 2)),
        dma((chunks, 2)), dma((chunks, 2)),
        dma((chunks, 2, nz)), dma((ITERS, chunks, 2, nz)),
        dma((chunks, nx - 1)), dma((ITERS, chunks, nx - 1)),
        dma((chunks,)), dma((ITERS, chunks)),
        dma((chunks, ny - 1)), dma((ITERS, chunks, ny - 1)),
        dma((chunks, nz - 1)), dma((ITERS, chunks, nz - 1)),
        dma((nz - 1,)), dma((nz - 1,)),
        dma((nx - 1,)), dma((nx - 1,)),
        dma((1,)), dma((1,)),
        dma((2,)), dma((2,)),
        dma((nx - 1,)), dma((nx - 1,)),
        dma((1,)), dma((1,)),
        dma((nz - 1,)), dma((nz - 1,)),
        dma((nz - 1,)), dma((nz - 1,)),
        dma((ny - 1,)), dma((ny - 1,)),
        dma((2,)), dma((2,)),
    ]
    anywhere = pl.BlockSpec(memory_space=pl.ANY)
    out = jax.ShapeDtypeStruct((unknowns, cases), F32)
    sol, res = pl.pallas_call(
        functools.partial(kernel, nx, nz, ny, chunks),
        out_shape=(out, out),
        in_specs=[pl.BlockSpec(memory_space=pltpu.SMEM)] * 2
        + [pl.BlockSpec(memory_space=pltpu.VMEM)]
        + [anywhere] * 5,
        out_specs=(anywhere, anywhere),
        scratch_shapes=scratch,
        compiler_params=pltpu.CompilerParams(
            collective_id=0, has_side_effects=True, vmem_limit_bytes=56 * 1024 * 1024
        ),
        cost_estimate=pl.CostEstimate(flops=2 * 9 * unknowns * unknowns * cases, bytes_accessed=1 << 24, transcendentals=0),
    )(
        shared_sizes[0, 0],
        stiffness[0],
        coarse_dofs[0],
        load_cases[0, 0],
        schur_blocks[0, 0],
        neumann_inverse[0, 0],
        coarse_basis[0, 0],
        coarse_inverse,
    )
    return (sol[None, None], res[None, None])


def solution(mesh):
    return jax.shard_map(
        on_device,
        mesh=mesh,
        in_specs=(
            P("group", "sub", None),
            P("group", "sub"),
            P("group", "sub", None, None),
            P("group", "sub", None, None),
            P("group", "sub", None, None),
            P("group", "sub", None, None),
            P("group", "sub", None),
            P("sub", None),
        ),
        out_specs=(P("group", "sub", None, None), P("group", "sub", None, None)),
        check_vma=False,
    )
```

```python
import functools
import math

import jax
import jax.numpy as jnp
from jax import lax
from jax.experimental import pallas as pl
from jax.experimental.pallas import tpu as pltpu
from jax.sharding import PartitionSpec as P

ITERS = 4
OMEGA = 0.6
SH = 256
COLS = 128
CORES = 2
F32 = jnp.float32
BF16 = jnp.bfloat16


def iota(shape, dim):
    return lax.broadcasted_iota(jnp.int32, shape, dim)


def kernel(
    nx, nz, ny, chunks,
    share, stiff, dofs, loads_hbm, schur_hbm, neumann_hbm, basis_hbm, coarse_hbm,
    sol_hbm, res_hbm,
    schur, neumann, basis, coarse, halves,
    loads, local, field, sol, weighted, rounded,
    from_lower, from_upper, corr_lower, corr_upper,
    weight_head, weight_tail, perm, perm_t,
    edge_out, edge_in, extended, extended_t,
    pick_rows, select, chosen, columns, columns_hl, coarse_k, coarse_part,
    terms, part_y, got_y, part_z, got_z, near_z,
    facts, facts_near, facts_far, facts_side,
    loc_sem, out_sem,
    h1s, h1r, h2s, h2r, nps, npr, xs, xr, cs, cr, ys, yr, zs, zr,
    gzs, gzr, gxs, gxr, gcs, gcr, bs, br,
    fxs, fxr, fcs, fcr, fzs, fzr, fbs, fbr, fys, fyr, fns, fnr,
):
    half = nz // CORES
    subs = nx * nz
    unknowns = loads.shape[1]
    ncl = basis.shape[0]
    order = coarse.shape[1]
    own_rows = coarse.shape[0]
    tail0 = unknowns - SH
    tiles = unknowns // SH
    edges = (0, tiles - 1)
    inner = tuple(range(1, tiles - 1))

    g, s = lax.axis_index("group"), lax.axis_index("sub")
    y, c = g // CORES, g % CORES
    z, x = s // nx, s % nx
    upper = (g, lax.rem(s + 1, subs))
    lower = (g, lax.rem(s + subs - 1, subs))
    x_peers = [(g, z * nx + lax.rem(x + d, nx)) for d in range(1, nx)]
    z_peers = [(g, lax.rem(z + d, nz) * nx + x) for d in range(1, nz)]
    in_column = [lax.rem(z + d, nz) * nx + x for d in range(nz)]
    beside = [[(g, lax.rem(sub + step, subs)) for sub in in_column] for step in (1, subs - 1)]
    y_peers = [(lax.rem(y + d, ny) * CORES + c, s) for d in range(1, ny)]
    core_peer = (y * CORES + 1 - c, s)

    share_low, share_up = share[0], share[1]

    def remote(src, dst, send, recv, to):
        return pltpu.make_async_remote_copy(
            src_ref=src, dst_ref=dst, send_sem=send, recv_sem=recv,
            device_id=to, device_id_type=pl.DeviceIdType.MESH,
        )

    def start(copies):
        for copy in copies:
            copy.start()

    def landed(copies):
        for copy in copies:
            copy.wait_recv()

    def sent(copies):
        for copy in copies:
            copy.wait_send()

    def rows(tile):
        return pl.ds(tile * SH, SH)

    def halo_local(ch):
        return (
            remote(local.at[ch, pl.ds(tail0, SH)], from_lower.at[ch], h1s.at[ch, 0], h1r.at[ch, 0], upper),
            remote(local.at[ch, pl.ds(0, SH)], from_upper.at[ch], h1s.at[ch, 1], h1r.at[ch, 1], lower),
        )

    def halo_field(ch):
        return (
            remote(field.at[ch, pl.ds(tail0, SH)], corr_lower.at[ch], h2s.at[ch, 0], h2r.at[ch, 0], upper),
            remote(field.at[ch, pl.ds(0, SH)], corr_upper.at[ch], h2s.at[ch, 1], h2r.at[ch, 1], lower),
        )

    def terms_x(k, ch):
        own = terms.at[k, ch, c, x]
        return [remote(own, own, xs.at[ch, d], xr.at[k, ch, d], to) for d, to in enumerate(x_peers)]

    def terms_core(k, ch):
        own = terms.at[k, ch, c]
        return (remote(own, own, cs.at[ch], cr.at[k, ch], core_peer),)

    def parts_y(k, ch):
        return [
            remote(part_y.at[ch, lax.rem(y + d + 1, ny)], got_y.at[k, ch, d], ys.at[ch, d], yr.at[k, ch, d], to)
            for d, to in enumerate(y_peers)
        ]

    def parts_z(k, ch):
        return [
            remote(part_z.at[ch, lax.rem(z + d + 1, nz)], got_z.at[k, ch, z], zs.at[ch, d], zr.at[k, ch, d], to)
            for d, to in enumerate(z_peers)
        ]

    def parts_beside(k, ch):
        return [
            remote(
                part_z.at[ch, lax.rem(z + d, nz)], near_z.at[k, ch, side, z],
                nps.at[ch, side, d], npr.at[k, ch, side, d], beside[side][d],
            )
            for side in range(2)
            for d in range(nz)
        ]

    def basis_halo():
        return (
            remote(edge_out.at[0], edge_in.at[0], bs.at[0], br.at[0], upper),
            remote(edge_out.at[1], edge_in.at[1], bs.at[1], br.at[1], lower),
        )

    def columns_z():
        return [
            remote(chosen.at[lax.rem(z + d + 1, nz)], columns.at[c, x, lax.rem(z, half)], gzs.at[d], gzr.at[d], to)
            for d, to in enumerate(z_peers)
        ]

    def columns_x():
        own = columns.at[c, x]
        return [remote(own, own, gxs.at[d], gxr.at[d], to) for d, to in enumerate(x_peers)]

    def columns_core(j):
        own = columns.at[c, lax.rem(x + nx - j, nx)]
        return remote(own, own, gcs.at[j], gcr.at[j], core_peer)

    def facts_x():
        own = facts_near.at[z, c, x]
        return [remote(facts, own, fxs.at[d], fxr.at[d], to) for d, to in enumerate(x_peers)]

    def facts_core():
        own = facts_near.at[z, c]
        return (remote(own, own, fcs.at[0], fcr.at[0], core_peer),)

    def facts_z():
        own = facts_near.at[z]
        return [remote(own, own, fzs.at[d], fzr.at[d], to) for d, to in enumerate(z_peers)]

    def far_z():
        return [remote(facts, facts_far.at[y, z], fbs.at[d], fbr.at[d], to) for d, to in enumerate(z_peers)]

    def far_y():
        own = facts_far.at[y]
        return [remote(own, own, fys.at[d], fyr.at[d], to) for d, to in enumerate(y_peers)]

    def facts_beside():
        return (
            remote(facts, facts_side.at[0], fns.at[0], fnr.at[0], upper),
            remote(facts, facts_side.at[1], fns.at[1], fnr.at[1], lower),
        )

    load_in = [
        pltpu.make_async_copy(loads_hbm.at[:, pl.ds(ch * COLS, COLS)], loads.at[ch], loc_sem.at[ch])
        for ch in range(chunks)
    ]
    others = [
        pltpu.make_async_copy(src, dst, loc_sem.at[chunks + i])
        for i, (src, dst) in enumerate(
            ((basis_hbm, basis), (coarse_hbm, coarse), (neumann_hbm, neumann), (schur_hbm, schur))
        )
    ]
    start(load_in)
    start(others)
    facts[...] = jnp.full(facts.shape, stiff[0], F32)
    facts[0:1, :ncl] = dofs[...].astype(F32)
    facts_near[z, c, x] = facts[...]
    facts_far[y, z] = facts[...]
    barrier = pltpu.get_barrier_semaphore()
    peers = [*beside[0], *beside[1], *x_peers, *z_peers, *y_peers, core_peer]
    for peer in peers:
        pl.semaphore_signal(barrier, inc=1, device_id=peer, device_id_type=pl.DeviceIdType.MESH)

    turn = lax.rem(share_up, SH)
    turn_back = lax.rem(2 * SH - share_up, SH)
    moved = (iota((SH, SH), 0) + (SH - share_up)) & (SH - 1)
    perm[...] = jnp.where(iota((SH, SH), 1) == moved, 1.0, 0.0).astype(BF16)
    moved_lane = (iota((SH, SH), 1) + (SH - share_up)) & (SH - 1)
    perm_t[...] = jnp.where(iota((SH, SH), 0) == moved_lane, 1.0, 0.0).astype(BF16)
    for ch in range(chunks):
        load_in[ch].wait()
        loads[ch, tail0:, :] = pltpu.roll(loads[ch, tail0:, :], turn, axis=0)
        local[ch, :, :] = loads[ch, :, :]
    others[1].wait()
    high = coarse[...].astype(BF16)
    halves[0:own_rows, :] = high
    halves[own_rows:, :] = (coarse[...] - high.astype(F32)).astype(BF16)

    pl.semaphore_wait(barrier, len(peers))
    start(facts_x())
    start(facts_beside())
    start(far_z())
    for ch in range(chunks):
        start(halo_local(ch))

    landed(facts_x())
    start(facts_core())
    landed(facts_core())
    start(facts_z())
    landed(far_z())
    start(far_y())
    landed(facts_beside())
    own_stiff = facts[1:2, 0:1]
    low_stiff = facts_side[0, 1:2, 0:1]
    up_stiff = facts_side[1, 1:2, 0:1]
    w_low = own_stiff / (own_stiff + low_stiff)
    w_up = own_stiff / (own_stiff + up_stiff)
    n_low = low_stiff / (low_stiff + own_stiff)
    n_up = up_stiff / (up_stiff + own_stiff)
    in_low = iota((SH, COLS), 0) < share_low
    in_up = iota((SH, COLS), 0) < share_up
    weight_head[...] = jnp.where(in_low, w_low, 1.0)
    weight_tail[...] = jnp.where(in_up, w_up, 1.0)

    others[0].wait()
    basis_tail = jnp.dot(basis[:, tail0:], perm_t[...], preferred_element_type=F32)
    basis[:, tail0:] = basis_tail.astype(BF16)
    edge_out[0] = basis_tail
    edge_out[1] = basis[:, :SH].astype(F32)
    start(basis_halo())
    lane_low = iota((ncl, SH), 1) < share_low
    lane_up = iota((ncl, SH), 1) < share_up
    extended[...] = jnp.zeros_like(extended)
    extended[0:ncl, :] = basis[...].astype(F32)
    extended[0:ncl, :SH] = jnp.where(lane_low, w_low, 1.0) * extended[0:ncl, :SH]
    extended[0:ncl, tail0:] = jnp.where(lane_up, w_up, 1.0) * extended[0:ncl, tail0:]

    def dof_column(row):
        row = jnp.broadcast_to(row, (ncl, COLS))
        hit = iota((ncl, COLS), 0) == iota((ncl, COLS), 1)
        return jnp.sum(jnp.where(hit, row, 0.0), axis=1, keepdims=True).astype(jnp.int32)


    def choose(zt):
        row = jnp.concatenate(
            [facts_near[zt, cc, xx, 0:1, :ncl] for cc in range(CORES) for xx in range(nx)], axis=1
        ).astype(jnp.int32)

        def hot(part, carry):
            at = pl.ds(pl.multiple_of(part * SH, SH), SH)
            index = iota((SH, row.shape[1]), 0) + part * SH
            select[at, :] = jnp.where(index == row, 1.0, 0.0).astype(BF16)
            return carry

        lax.fori_loop(0, order // SH, hot, 0)
        both = jnp.dot(halves[...], select[...], preferred_element_type=F32)
        chosen[zt] = both[:own_rows] + both[own_rows:]

    sends_here = z // half == c
    choose(z)
    landed(facts_z())
    for d, copy in enumerate(columns_z()):
        choose(lax.rem(z + d + 1, nz))
        pl.when(sends_here)(copy.start)

    @pl.when(sends_here)
    def _():
        columns[c, x, lax.rem(z, half)] = chosen[z]

    edge = basis_halo()
    landed(edge)
    extended[ncl : 2 * ncl, :SH] = jnp.where(lane_low, n_low * edge_in[0], 0.0)
    extended[2 * ncl : 3 * ncl, tail0:] = jnp.where(lane_up, n_up * edge_in[1], 0.0)
    low = extended[...] - extended[...].astype(BF16).astype(F32)
    extended_t[:, :COLS] = extended[...].T.astype(BF16)
    extended_t[:, COLS:] = low.T.astype(BF16)
    sent(edge)
    landed(far_y())
    for yy in range(ny):
        for zz in range(nz):
            column = jnp.broadcast_to(dof_column(facts_far[yy, zz, 0:1, :]), (ncl, order))
            at = (yy * nz + zz) * ncl
            pick_rows[at : at + ncl, :] = jnp.where(iota((ncl, order), 1) == column, 1.0, 0.0).astype(BF16)

    def align(matrix):
        wide = jnp.dot(perm[...], matrix[tail0:, :], preferred_element_type=F32)
        matrix[tail0:, :] = wide.astype(BF16)

        def turn_columns(tile, carry):
            at = pl.ds(pl.multiple_of(tile * SH, SH), SH)
            swapped = jnp.dot(matrix[at, tail0:], perm_t[...], preferred_element_type=F32)
            matrix[at, tail0:] = swapped.astype(BF16)
            return carry

        lax.fori_loop(0, tiles, turn_columns, 0)

    others[2].wait()
    align(neumann)

    for d, copy in enumerate(columns_z()):
        sender = lax.rem(z + nz - 1 - d, nz)
        pl.when(sender // half == c)(copy.wait_recv)
    start(columns_x())
    columns_core(0).start()

    others[3].wait()
    align(schur)

    @pl.when(sends_here)
    def _():
        sent(columns_z())

    sol[...] = jnp.zeros_like(sol)
    for copies in (facts_beside(), facts_x(), far_z(), facts_core(), far_y(), facts_z()):
        sent(copies)

    def weigh(k, ch):
        landed(halo_local(ch))
        head = local[ch, :SH, :] + jnp.where(in_low, from_lower[ch], 0.0)
        weighted[ch, :SH, :] = (weight_head[...] * head).astype(BF16)
        weighted[ch, SH:tail0, :] = local[ch, SH:tail0, :].astype(BF16)
        tail = local[ch, tail0:, :] + jnp.where(in_up, from_upper[ch], 0.0)
        weighted[ch, tail0:, :] = (weight_tail[...] * tail).astype(BF16)
        terms[k, ch, c, x] = jnp.dot(basis[...], weighted[ch], preferred_element_type=F32)
        start(terms_x(k, ch))

    def precondition(k, ch):
        for tile in edges + inner:
            product = jnp.dot(neumann[rows(tile), :], weighted[ch], preferred_element_type=F32)
            if tile == 0:
                product = weight_head[...] * product
            if tile == tiles - 1:
                product = weight_tail[...] * product
            field[ch, rows(tile), :] = product
            if tile == edges[-1]:
                start(halo_field(ch))

    def to_core(k, ch):
        landed(terms_x(k, ch))
        start(terms_core(k, ch))

    def solve(k, ch):
        landed(terms_core(k, ch))
        mine = terms[k, ch].reshape(CORES * nx * ncl, COLS)
        high = mine.astype(BF16)
        low = (mine - high.astype(F32)).astype(BF16)
        stacked = jnp.concatenate([high, high, low], axis=0)
        solved = jnp.dot(coarse_k[...], stacked, preferred_element_type=F32)
        part_y[ch] = solved.reshape(ny, nz * ncl, COLS)
        start(parts_y(k, ch))

    def sum_y(k, ch):
        copies = parts_y(k, ch)
        landed(copies)
        whole = part_y[ch, y]
        for d in range(ny - 1):
            whole = whole + got_y[k, ch, d]
        part_z[ch] = whole.reshape(nz, ncl, COLS)
        got_z[k, ch, z] = part_z[ch, z]
        start(parts_z(k, ch) + parts_beside(k, ch))
        sent(copies)

    def total(parts):
        result = parts[0]
        for i in range(1, nz):
            result = result + parts[i]
        return result

    def advance(k, ch):
        parts = parts_z(k, ch) + parts_beside(k, ch)
        landed(parts)
        halo = halo_field(ch)
        landed(halo)
        stacked = jnp.concatenate(
            [total(got_z.at[k, ch]), total(near_z.at[k, ch, 0]), total(near_z.at[k, ch, 1]), jnp.zeros((COLS - 3 * ncl, COLS), F32)], axis=0
        ).astype(BF16)
        stacked = jnp.concatenate([stacked, stacked], axis=0)
        sent(parts)
        sent(halo)
        for tile in range(tiles):
            change = field[ch, rows(tile), :] + jnp.dot(
                extended_t[rows(tile), :], stacked, preferred_element_type=F32
            )
            if tile == 0:
                change = change + jnp.where(in_low, corr_lower[ch], 0.0)
            if tile == tiles - 1:
                change = change + jnp.where(in_up, corr_upper[ch], 0.0)
            new = sol[ch, rows(tile), :] + OMEGA * change
            sol[ch, rows(tile), :] = new
            rounded[rows(tile), :] = new.astype(BF16)
        out = halo_local(ch)
        sent(out)
        for tile in edges + inner:
            product = jnp.dot(schur[rows(tile), :], rounded[...], preferred_element_type=F32)
            local[ch, rows(tile), :] = loads[ch, rows(tile), :] - product
            if tile == edges[-1]:
                start(out)
        sent(terms_x(k, ch))
        sent(terms_core(k, ch))

    wide = CORES * nx * ncl
    depth = nx * half * own_rows

    def split_slot(cc, slot):
        for i in range(half):
            block = columns[cc, slot, i]
            high = block.astype(BF16)
            at = pl.ds(pl.multiple_of(((cc * half + i) * nx + slot) * own_rows, own_rows), own_rows)
            columns_hl[at, :wide] = high
            columns_hl[at, wide:] = (block - high.astype(F32)).astype(BF16)

    def pick_half(cc, finish):
        step = min(SH, pick_rows.shape[0])
        inside = pl.ds(pl.multiple_of(cc * depth, depth), depth)

        def row_tile(tile, carry):
            at = pl.ds(pl.multiple_of(tile * step, step), step)
            both = jnp.dot(pick_rows[at, inside], columns_hl[inside, :], preferred_element_type=F32)
            if not finish:
                coarse_part[at, :] = both
                return carry
            both = both + coarse_part[at, :]
            high = both[:, :wide].astype(BF16)
            coarse_k[at, :wide] = high
            coarse_k[at, wide : 2 * wide] = both[:, wide:].astype(BF16)
            coarse_k[at, 2 * wide :] = high
            return carry

        lax.fori_loop(0, pick_rows.shape[0] // step, row_tile, 0)

    def finish_setup():
        to_peer = [columns_core(j) for j in range(nx)]
        split_slot(c, x)
        for d, copy in enumerate(columns_x()):
            copy.wait_recv()
            to_peer[d + 1].start()
            split_slot(c, lax.rem(x + nx - d - 1, nx))
        pick_half(c, False)
        landed(to_peer)
        for slot in range(nx):
            split_slot(1 - c, slot)
        pick_half(1 - c, True)
        sent(columns_x())
        sent(to_peer)

    def each_chunk(step):
        def body(ch, carry):
            step(0, ch)
            return carry

        lax.fori_loop(0, chunks, body, 0)

    lanes = chunks + 2

    def tick(now, carry):
        def run(step, late, first=0):
            turn = now - late

            @pl.when((turn >= first * lanes) & (turn < ITERS * lanes) & (lax.rem(turn + lanes, lanes) < chunks))
            def _():
                step(turn // lanes, lax.rem(turn, lanes))

        run(weigh, 0, 1)
        run(to_core, 1, 1)
        run(sum_y, 2)
        run(solve, 1)
        run(precondition, 0, 1)
        run(advance, 3)
        return carry

    each_chunk(weigh)
    each_chunk(precondition)
    each_chunk(to_core)
    finish_setup()
    lax.fori_loop(1, ITERS * lanes + 3 - 1, tick, 0)

    out_copies = []
    for ch in range(chunks):
        sol[ch, tail0:, :] = pltpu.roll(sol[ch, tail0:, :], turn_back, axis=0)
        copy = pltpu.make_async_copy(sol.at[ch], sol_hbm.at[:, pl.ds(ch * COLS, COLS)], out_sem.at[ch])
        copy.start()
        out_copies.append(copy)
    for ch in range(chunks):
        copies = halo_local(ch)
        landed(copies)
        field[ch, :SH, :] = local[ch, :SH, :] + jnp.where(in_low, from_lower[ch], 0.0)
        field[ch, SH:tail0, :] = local[ch, SH:tail0, :]
        tail = local[ch, tail0:, :] + jnp.where(in_up, from_upper[ch], 0.0)
        field[ch, tail0:, :] = pltpu.roll(tail, turn_back, axis=0)
        copy = pltpu.make_async_copy(field.at[ch], res_hbm.at[:, pl.ds(ch * COLS, COLS)], out_sem.at[chunks + ch])
        copy.start()
        out_copies.append(copy)
        sent(copies)
    for copy in out_copies:
        copy.wait()


def on_device(
    shared_sizes,
    stiffness,
    load_cases,
    schur_blocks,
    neumann_inverse,
    coarse_basis,
    coarse_dofs,
    coarse_inverse,
):
    groups, subs = lax.axis_size("group"), lax.axis_size("sub")
    nx = math.isqrt(subs)
    nz, ny = subs // nx, groups // CORES
    half = nz // CORES
    unknowns, cases = load_cases.shape[2:]
    chunks = cases // COLS
    ncl = coarse_basis.shape[2]
    own_rows, order = coarse_inverse.shape
    wide, tall = CORES * nx * ncl, ny * nz * ncl

    dma = pltpu.SemaphoreType.DMA
    vmem = pltpu.VMEM
    scratch = [
        vmem((unknowns, unknowns), BF16),
        vmem((unknowns, unknowns), BF16),
        vmem((ncl, unknowns), BF16),
        vmem((own_rows, order), F32),
        vmem((2 * own_rows, order), BF16),
        vmem((chunks, unknowns, COLS), F32),
        vmem((chunks, unknowns, COLS), F32),
        vmem((chunks, unknowns, COLS), F32),
        vmem((chunks, unknowns, COLS), F32),
        vmem((chunks, unknowns, COLS), BF16),
        vmem((unknowns, COLS), BF16),
        vmem((chunks, SH, COLS), F32),
        vmem((chunks, SH, COLS), F32),
        vmem((chunks, SH, COLS), F32),
        vmem((chunks, SH, COLS), F32),
        vmem((SH, COLS), F32),
        vmem((SH, COLS), F32),
        vmem((SH, SH), BF16),
        vmem((SH, SH), BF16),
        vmem((2, ncl, SH), F32),
        vmem((2, ncl, SH), F32),
        vmem((COLS, unknowns), F32),
        vmem((unknowns, 2 * COLS), BF16),
        vmem((tall, order), BF16),
        vmem((order, wide), BF16),
        vmem((nz, own_rows, wide), F32),
        vmem((CORES, nx, half, own_rows, wide), F32),
        vmem((order, 2 * wide), BF16),
        vmem((tall, 3 * wide), BF16),
        vmem((tall, 2 * wide), F32),
        vmem((ITERS, chunks, CORES, nx, ncl, COLS), F32),
        vmem((chunks, ny, nz * ncl, COLS), F32),
        vmem((ITERS, chunks, ny - 1, nz * ncl, COLS), F32),
        vmem((chunks, nz, ncl, COLS), F32),
        vmem((ITERS, chunks, nz, ncl, COLS), F32),
        vmem((ITERS, chunks, 2, nz, ncl, COLS), F32),
        vmem((8, COLS), F32),
        vmem((nz, CORES, nx, 8, COLS), F32),
        vmem((ny, nz, 8, COLS), F32),
        vmem((2, 8, COLS), F32),
        dma((chunks + 4,)),
        dma((2 * chunks,)),
        dma((chunks, 2)), dma((chunks, 2)),
        dma((chunks, 2)), dma((chunks, 2)),
        dma((chunks, 2, nz)), dma((ITERS, chunks, 2, nz)),
        dma((chunks, nx - 1)), dma((ITERS, chunks, nx - 1)),
        dma((chunks,)), dma((ITERS, chunks)),
        dma((chunks, ny - 1)), dma((ITERS, chunks, ny - 1)),
        dma((chunks, nz - 1)), dma((ITERS, chunks, nz - 1)),
        dma((nz - 1,)), dma((nz - 1,)),
        dma((nx - 1,)), dma((nx - 1,)),
        dma((nx,)), dma((nx,)),
        dma((2,)), dma((2,)),
        dma((nx - 1,)), dma((nx - 1,)),
        dma((1,)), dma((1,)),
        dma((nz - 1,)), dma((nz - 1,)),
        dma((nz - 1,)), dma((nz - 1,)),
        dma((ny - 1,)), dma((ny - 1,)),
        dma((2,)), dma((2,)),
    ]
    anywhere = pl.BlockSpec(memory_space=pl.ANY)
    out = jax.ShapeDtypeStruct((unknowns, cases), F32)
    sol, res = pl.pallas_call(
        functools.partial(kernel, nx, nz, ny, chunks),
        out_shape=(out, out),
        in_specs=[pl.BlockSpec(memory_space=pltpu.SMEM)] * 2
        + [pl.BlockSpec(memory_space=pltpu.VMEM)]
        + [anywhere] * 5,
        out_specs=(anywhere, anywhere),
        scratch_shapes=scratch,
        compiler_params=pltpu.CompilerParams(
            collective_id=0, has_side_effects=True, vmem_limit_bytes=56 * 1024 * 1024
        ),
        cost_estimate=pl.CostEstimate(flops=2 * 9 * unknowns * unknowns * cases, bytes_accessed=1 << 24, transcendentals=0),
    )(
        shared_sizes[0, 0],
        stiffness[0],
        coarse_dofs[0],
        load_cases[0, 0],
        schur_blocks[0, 0],
        neumann_inverse[0, 0],
        coarse_basis[0, 0],
        coarse_inverse,
    )
    return (sol[None, None], res[None, None])


def solution(mesh):
    return jax.shard_map(
        on_device,
        mesh=mesh,
        in_specs=(
            P("group", "sub", None),
            P("group", "sub"),
            P("group", "sub", None, None),
            P("group", "sub", None, None),
            P("group", "sub", None, None),
            P("group", "sub", None, None),
            P("group", "sub", None),
            P("sub", None),
        ),
        out_specs=(P("group", "sub", None, None), P("group", "sub", None, None)),
        check_vma=False,
    )
```

```python
import functools
import math

import jax
import jax.numpy as jnp
from jax import lax
from jax.experimental import pallas as pl
from jax.experimental.pallas import tpu as pltpu
from jax.sharding import PartitionSpec as P

ITERS = 4
OMEGA = 0.6
SH = 256
COLS = 128
CORES = 2
F32 = jnp.float32
BF16 = jnp.bfloat16


def iota(shape, dim):
    return lax.broadcasted_iota(jnp.int32, shape, dim)


def kernel(
    nx, nz, ny, chunks,
    share, stiff, dofs, loads_hbm, schur_hbm, neumann_hbm, basis_hbm, coarse_hbm,
    sol_hbm, res_hbm,
    schur, neumann, basis, coarse, halves,
    loads, local, field, sol, weighted, rounded,
    from_lower, from_upper, corr_lower, corr_upper,
    weight_head, weight_tail, perm, perm_t,
    edge_out, edge_in, extended, extended_t,
    pick_rows, select, chosen, columns, columns_hl, coarse_k, coarse_part,
    terms, part_y, got_y, part_z, got_z, near_z,
    facts, facts_near, facts_far, facts_side,
    loc_sem, out_sem,
    h1s, h1r, h2s, h2r, nps, npr, xs, xr, cs, cr, ys, yr, zs, zr,
    gzs, gzr, gxs, gxr, gcs, gcr, bs, br,
    fxs, fxr, fcs, fcr, fzs, fzr, fbs, fbr, fys, fyr, fns, fnr,
):
    half = nz // CORES
    subs = nx * nz
    unknowns = loads.shape[1]
    ncl = basis.shape[0]
    order = coarse.shape[1]
    own_rows = coarse.shape[0]
    tail0 = unknowns - SH
    tiles = unknowns // SH
    edges = (0, tiles - 1)
    inner = tuple(range(1, tiles - 1))

    g, s = lax.axis_index("group"), lax.axis_index("sub")
    y, c = g // CORES, g % CORES
    z, x = s // nx, s % nx
    upper = (g, lax.rem(s + 1, subs))
    lower = (g, lax.rem(s + subs - 1, subs))
    x_peers = [(g, z * nx + lax.rem(x + d, nx)) for d in range(1, nx)]
    z_peers = [(g, lax.rem(z + d, nz) * nx + x) for d in range(1, nz)]
    in_column = [lax.rem(z + d, nz) * nx + x for d in range(nz)]
    beside = [[(g, lax.rem(sub + step, subs)) for sub in in_column] for step in (1, subs - 1)]
    y_peers = [(lax.rem(y + d, ny) * CORES + c, s) for d in range(1, ny)]
    core_peer = (y * CORES + 1 - c, s)

    share_low, share_up = share[0], share[1]

    def remote(src, dst, send, recv, to):
        return pltpu.make_async_remote_copy(
            src_ref=src, dst_ref=dst, send_sem=send, recv_sem=recv,
            device_id=to, device_id_type=pl.DeviceIdType.MESH,
        )

    def start(copies):
        for copy in copies:
            copy.start()

    def landed(copies):
        for copy in copies:
            copy.wait_recv()

    def sent(copies):
        for copy in copies:
            copy.wait_send()

    def rows(tile):
        return pl.ds(tile * SH, SH)

    def halo_local(ch):
        return (
            remote(local.at[ch, pl.ds(tail0, SH)], from_lower.at[ch], h1s.at[ch, 0], h1r.at[ch, 0], upper),
            remote(local.at[ch, pl.ds(0, SH)], from_upper.at[ch], h1s.at[ch, 1], h1r.at[ch, 1], lower),
        )

    def halo_field(ch):
        return (
            remote(field.at[ch, pl.ds(tail0, SH)], corr_lower.at[ch], h2s.at[ch, 0], h2r.at[ch, 0], upper),
            remote(field.at[ch, pl.ds(0, SH)], corr_upper.at[ch], h2s.at[ch, 1], h2r.at[ch, 1], lower),
        )

    def terms_x(k, ch):
        own = terms.at[k, ch, c, x]
        return [remote(own, own, xs.at[ch, d], xr.at[k, ch, d], to) for d, to in enumerate(x_peers)]

    def terms_core(k, ch):
        own = terms.at[k, ch, c]
        return (remote(own, own, cs.at[ch], cr.at[k, ch], core_peer),)

    def parts_y(k, ch):
        return [
            remote(part_y.at[ch, lax.rem(y + d + 1, ny)], got_y.at[k, ch, d], ys.at[ch, d], yr.at[k, ch, d], to)
            for d, to in enumerate(y_peers)
        ]

    def parts_z(k, ch):
        return [
            remote(part_z.at[ch, lax.rem(z + d + 1, nz)], got_z.at[k, ch, z], zs.at[ch, d], zr.at[k, ch, d], to)
            for d, to in enumerate(z_peers)
        ]

    def parts_beside(k, ch):
        return [
            remote(
                part_z.at[ch, lax.rem(z + d, nz)], near_z.at[k, ch, side, z],
                nps.at[ch, side, d], npr.at[k, ch, side, d], beside[side][d],
            )
            for side in range(2)
            for d in range(nz)
        ]

    def basis_halo():
        return (
            remote(edge_out.at[0], edge_in.at[0], bs.at[0], br.at[0], upper),
            remote(edge_out.at[1], edge_in.at[1], bs.at[1], br.at[1], lower),
        )

    def columns_z():
        return [
            remote(chosen.at[lax.rem(z + d + 1, nz)], columns.at[c, x, lax.rem(z, half)], gzs.at[d], gzr.at[d], to)
            for d, to in enumerate(z_peers)
        ]

    def columns_x(i):
        own = columns.at[c, x, i]
        return [remote(own, own, gxs.at[d, i], gxr.at[d, i], to) for d, to in enumerate(x_peers)]

    def columns_core(j):
        own = columns.at[c, lax.rem(x + nx - j, nx)]
        return remote(own, own, gcs.at[j], gcr.at[j], core_peer)

    def facts_x():
        own = facts_near.at[z, c, x]
        return [remote(facts, own, fxs.at[d], fxr.at[d], to) for d, to in enumerate(x_peers)]

    def facts_core():
        own = facts_near.at[z, c]
        return (remote(own, own, fcs.at[0], fcr.at[0], core_peer),)

    def facts_z():
        own = facts_near.at[z]
        return [remote(own, own, fzs.at[d], fzr.at[d], to) for d, to in enumerate(z_peers)]

    def far_z():
        return [remote(facts, facts_far.at[y, z], fbs.at[d], fbr.at[d], to) for d, to in enumerate(z_peers)]

    def far_y():
        own = facts_far.at[y]
        return [remote(own, own, fys.at[d], fyr.at[d], to) for d, to in enumerate(y_peers)]

    def facts_beside():
        return (
            remote(facts, facts_side.at[0], fns.at[0], fnr.at[0], upper),
            remote(facts, facts_side.at[1], fns.at[1], fnr.at[1], lower),
        )

    load_in = [
        pltpu.make_async_copy(loads_hbm.at[:, pl.ds(ch * COLS, COLS)], loads.at[ch], loc_sem.at[ch])
        for ch in range(chunks)
    ]
    others = [
        pltpu.make_async_copy(src, dst, loc_sem.at[chunks + i])
        for i, (src, dst) in enumerate(
            ((basis_hbm, basis), (coarse_hbm, coarse), (neumann_hbm, neumann), (schur_hbm, schur))
        )
    ]
    start(load_in)
    start(others)
    facts[...] = jnp.full(facts.shape, stiff[0], F32)
    facts[0:1, :ncl] = dofs[...].astype(F32)
    facts_near[z, c, x] = facts[...]
    facts_far[y, z] = facts[...]
    barrier = pltpu.get_barrier_semaphore()
    peers = [*beside[0], *beside[1], *x_peers, *z_peers, *y_peers, core_peer]
    for peer in peers:
        pl.semaphore_signal(barrier, inc=1, device_id=peer, device_id_type=pl.DeviceIdType.MESH)

    turn = lax.rem(share_up, SH)
    turn_back = lax.rem(2 * SH - share_up, SH)
    moved = (iota((SH, SH), 0) + (SH - share_up)) & (SH - 1)
    perm[...] = jnp.where(iota((SH, SH), 1) == moved, 1.0, 0.0).astype(BF16)
    moved_lane = (iota((SH, SH), 1) + (SH - share_up)) & (SH - 1)
    perm_t[...] = jnp.where(iota((SH, SH), 0) == moved_lane, 1.0, 0.0).astype(BF16)
    for ch in range(chunks):
        load_in[ch].wait()
        loads[ch, tail0:, :] = pltpu.roll(loads[ch, tail0:, :], turn, axis=0)
        local[ch, :, :] = loads[ch, :, :]
    others[1].wait()
    high = coarse[...].astype(BF16)
    halves[0:own_rows, :] = high
    halves[own_rows:, :] = (coarse[...] - high.astype(F32)).astype(BF16)

    pl.semaphore_wait(barrier, len(peers))
    start(facts_x())
    start(facts_beside())
    start(far_z())
    for ch in range(chunks):
        start(halo_local(ch))

    landed(facts_x())
    start(facts_core())
    landed(facts_core())
    start(facts_z())
    landed(far_z())
    start(far_y())
    landed(facts_beside())
    own_stiff = facts[1:2, 0:1]
    low_stiff = facts_side[0, 1:2, 0:1]
    up_stiff = facts_side[1, 1:2, 0:1]
    w_low = own_stiff / (own_stiff + low_stiff)
    w_up = own_stiff / (own_stiff + up_stiff)
    n_low = low_stiff / (low_stiff + own_stiff)
    n_up = up_stiff / (up_stiff + own_stiff)
    in_low = iota((SH, COLS), 0) < share_low
    in_up = iota((SH, COLS), 0) < share_up
    weight_head[...] = jnp.where(in_low, w_low, 1.0)
    weight_tail[...] = jnp.where(in_up, w_up, 1.0)

    others[0].wait()
    basis_tail = jnp.dot(basis[:, tail0:], perm_t[...], preferred_element_type=F32)
    basis[:, tail0:] = basis_tail.astype(BF16)
    edge_out[0] = basis_tail
    edge_out[1] = basis[:, :SH].astype(F32)
    start(basis_halo())
    lane_low = iota((ncl, SH), 1) < share_low
    lane_up = iota((ncl, SH), 1) < share_up
    extended[...] = jnp.zeros_like(extended)
    extended[0:ncl, :] = basis[...].astype(F32)
    extended[0:ncl, :SH] = jnp.where(lane_low, w_low, 1.0) * extended[0:ncl, :SH]
    extended[0:ncl, tail0:] = jnp.where(lane_up, w_up, 1.0) * extended[0:ncl, tail0:]

    def dof_column(row):
        row = jnp.broadcast_to(row, (ncl, COLS))
        hit = iota((ncl, COLS), 0) == iota((ncl, COLS), 1)
        return jnp.sum(jnp.where(hit, row, 0.0), axis=1, keepdims=True).astype(jnp.int32)


    def choose(zt):
        row = jnp.concatenate(
            [facts_near[zt, cc, xx, 0:1, :ncl] for cc in range(CORES) for xx in range(nx)], axis=1
        ).astype(jnp.int32)

        def hot(part, carry):
            at = pl.ds(pl.multiple_of(part * SH, SH), SH)
            index = iota((SH, row.shape[1]), 0) + part * SH
            select[at, :] = jnp.where(index == row, 1.0, 0.0).astype(BF16)
            return carry

        lax.fori_loop(0, order // SH, hot, 0)
        both = jnp.dot(halves[...], select[...], preferred_element_type=F32)
        chosen[zt] = both[:own_rows] + both[own_rows:]

    sends_here = z // half == c
    choose(z)

    @pl.when(sends_here)
    def _():
        columns[c, x, lax.rem(z, half)] = chosen[z]
        start(columns_x(lax.rem(z, half)))

    landed(facts_z())
    for d, copy in enumerate(columns_z()):
        choose(lax.rem(z + d + 1, nz))
        pl.when(sends_here)(copy.start)

    edge = basis_halo()
    landed(edge)
    extended[ncl : 2 * ncl, :SH] = jnp.where(lane_low, n_low * edge_in[0], 0.0)
    extended[2 * ncl : 3 * ncl, tail0:] = jnp.where(lane_up, n_up * edge_in[1], 0.0)
    low = extended[...] - extended[...].astype(BF16).astype(F32)
    extended_t[:, :COLS] = extended[...].T.astype(BF16)
    extended_t[:, COLS:] = low.T.astype(BF16)
    sent(edge)
    landed(far_y())
    for yy in range(ny):
        for zz in range(nz):
            column = jnp.broadcast_to(dof_column(facts_far[yy, zz, 0:1, :]), (ncl, order))
            at = (yy * nz + zz) * ncl
            pick_rows[at : at + ncl, :] = jnp.where(iota((ncl, order), 1) == column, 1.0, 0.0).astype(BF16)

    def align(matrix):
        wide = jnp.dot(perm[...], matrix[tail0:, :], preferred_element_type=F32)
        matrix[tail0:, :] = wide.astype(BF16)

        def turn_columns(tile, carry):
            at = pl.ds(pl.multiple_of(tile * SH, SH), SH)
            swapped = jnp.dot(matrix[at, tail0:], perm_t[...], preferred_element_type=F32)
            matrix[at, tail0:] = swapped.astype(BF16)
            return carry

        lax.fori_loop(0, tiles, turn_columns, 0)

    others[2].wait()
    align(neumann)

    for d, copy in enumerate(columns_z()):
        sender = lax.rem(z + nz - 1 - d, nz)
        pl.when(sender // half == c)(copy.wait_recv)
    for i in range(half):
        pl.when(c * half + i != z)(functools.partial(lambda i: start(columns_x(i)), i))
    columns_core(0).start()

    others[3].wait()
    align(schur)

    @pl.when(sends_here)
    def _():
        sent(columns_z())

    sol[...] = jnp.zeros_like(sol)
    for copies in (facts_beside(), facts_x(), far_z(), facts_core(), far_y(), facts_z()):
        sent(copies)

    def weigh(k, ch):
        landed(halo_local(ch))
        head = local[ch, :SH, :] + jnp.where(in_low, from_lower[ch], 0.0)
        weighted[ch, :SH, :] = (weight_head[...] * head).astype(BF16)
        weighted[ch, SH:tail0, :] = local[ch, SH:tail0, :].astype(BF16)
        tail = local[ch, tail0:, :] + jnp.where(in_up, from_upper[ch], 0.0)
        weighted[ch, tail0:, :] = (weight_tail[...] * tail).astype(BF16)
        terms[k, ch, c, x] = jnp.dot(basis[...], weighted[ch], preferred_element_type=F32)
        start(terms_x(k, ch))

    def precondition(k, ch):
        for tile in edges + inner:
            product = jnp.dot(neumann[rows(tile), :], weighted[ch], preferred_element_type=F32)
            if tile == 0:
                product = weight_head[...] * product
            if tile == tiles - 1:
                product = weight_tail[...] * product
            field[ch, rows(tile), :] = product
            if tile == edges[-1]:
                start(halo_field(ch))

    def to_core(k, ch):
        landed(terms_x(k, ch))
        start(terms_core(k, ch))

    def solve(k, ch):
        landed(terms_core(k, ch))
        mine = terms[k, ch].reshape(CORES * nx * ncl, COLS)
        high = mine.astype(BF16)
        low = (mine - high.astype(F32)).astype(BF16)
        stacked = jnp.concatenate([high, high, low], axis=0)
        solved = jnp.dot(coarse_k[...], stacked, preferred_element_type=F32)
        part_y[ch] = solved.reshape(ny, nz * ncl, COLS)
        start(parts_y(k, ch))

    def sum_y(k, ch):
        copies = parts_y(k, ch)
        landed(copies)
        whole = part_y[ch, y]
        for d in range(ny - 1):
            whole = whole + got_y[k, ch, d]
        part_z[ch] = whole.reshape(nz, ncl, COLS)
        got_z[k, ch, z] = part_z[ch, z]
        start(parts_z(k, ch) + parts_beside(k, ch))
        sent(copies)

    def total(parts):
        result = parts[0]
        for i in range(1, nz):
            result = result + parts[i]
        return result

    def advance(k, ch):
        parts = parts_z(k, ch) + parts_beside(k, ch)
        landed(parts)
        halo = halo_field(ch)
        landed(halo)
        stacked = jnp.concatenate(
            [total(got_z.at[k, ch]), total(near_z.at[k, ch, 0]), total(near_z.at[k, ch, 1]), jnp.zeros((COLS - 3 * ncl, COLS), F32)], axis=0
        ).astype(BF16)
        stacked = jnp.concatenate([stacked, stacked], axis=0)
        sent(parts)
        sent(halo)
        for tile in range(tiles):
            change = field[ch, rows(tile), :] + jnp.dot(
                extended_t[rows(tile), :], stacked, preferred_element_type=F32
            )
            if tile == 0:
                change = change + jnp.where(in_low, corr_lower[ch], 0.0)
            if tile == tiles - 1:
                change = change + jnp.where(in_up, corr_upper[ch], 0.0)
            new = sol[ch, rows(tile), :] + OMEGA * change
            sol[ch, rows(tile), :] = new
            rounded[rows(tile), :] = new.astype(BF16)
        out = halo_local(ch)
        sent(out)
        for tile in edges + inner:
            product = jnp.dot(schur[rows(tile), :], rounded[...], preferred_element_type=F32)
            local[ch, rows(tile), :] = loads[ch, rows(tile), :] - product
            if tile == edges[-1]:
                start(out)
        sent(terms_x(k, ch))
        sent(terms_core(k, ch))

    wide = CORES * nx * ncl
    depth = nx * half * own_rows

    def split_slot(cc, slot):
        for i in range(half):
            block = columns[cc, slot, i]
            high = block.astype(BF16)
            at = pl.ds(pl.multiple_of(((cc * half + i) * nx + slot) * own_rows, own_rows), own_rows)
            columns_hl[at, :wide] = high
            columns_hl[at, wide:] = (block - high.astype(F32)).astype(BF16)

    def pick_half(cc, finish):
        step = min(SH, pick_rows.shape[0])
        inside = pl.ds(pl.multiple_of(cc * depth, depth), depth)

        def row_tile(tile, carry):
            at = pl.ds(pl.multiple_of(tile * step, step), step)
            both = jnp.dot(pick_rows[at, inside], columns_hl[inside, :], preferred_element_type=F32)
            if not finish:
                coarse_part[at, :] = both
                return carry
            both = both + coarse_part[at, :]
            high = both[:, :wide].astype(BF16)
            coarse_k[at, :wide] = high
            coarse_k[at, wide : 2 * wide] = both[:, wide:].astype(BF16)
            coarse_k[at, 2 * wide :] = high
            return carry

        lax.fori_loop(0, pick_rows.shape[0] // step, row_tile, 0)

    def finish_setup():
        to_peer = [columns_core(j) for j in range(nx)]
        split_slot(c, x)
        pieces = [columns_x(i) for i in range(half)]
        for d in range(nx - 1):
            landed([piece[d] for piece in pieces])
            to_peer[d + 1].start()
            split_slot(c, lax.rem(x + nx - d - 1, nx))
        pick_half(c, False)
        landed(to_peer)
        for slot in range(nx):
            split_slot(1 - c, slot)
        pick_half(1 - c, True)
        for piece in pieces:
            sent(piece)
        sent(to_peer)

    def each_chunk(step):
        def body(ch, carry):
            step(0, ch)
            return carry

        lax.fori_loop(0, chunks, body, 0)

    lanes = chunks + 2

    def tick(now, carry):
        def run(step, late, first=0):
            turn = now - late

            @pl.when((turn >= first * lanes) & (turn < ITERS * lanes) & (lax.rem(turn + lanes, lanes) < chunks))
            def _():
                step(turn // lanes, lax.rem(turn, lanes))

        run(weigh, 0, 1)
        run(to_core, 1, 1)
        run(sum_y, 2)
        run(solve, 1)
        run(precondition, 0, 1)
        run(advance, 3)
        return carry

    each_chunk(weigh)
    each_chunk(precondition)
    each_chunk(to_core)
    finish_setup()
    lax.fori_loop(1, ITERS * lanes + 3 - 1, tick, 0)

    out_copies = []
    for ch in range(chunks):
        sol[ch, tail0:, :] = pltpu.roll(sol[ch, tail0:, :], turn_back, axis=0)
        copy = pltpu.make_async_copy(sol.at[ch], sol_hbm.at[:, pl.ds(ch * COLS, COLS)], out_sem.at[ch])
        copy.start()
        out_copies.append(copy)
    for ch in range(chunks):
        copies = halo_local(ch)
        landed(copies)
        field[ch, :SH, :] = local[ch, :SH, :] + jnp.where(in_low, from_lower[ch], 0.0)
        field[ch, SH:tail0, :] = local[ch, SH:tail0, :]
        tail = local[ch, tail0:, :] + jnp.where(in_up, from_upper[ch], 0.0)
        field[ch, tail0:, :] = pltpu.roll(tail, turn_back, axis=0)
        copy = pltpu.make_async_copy(field.at[ch], res_hbm.at[:, pl.ds(ch * COLS, COLS)], out_sem.at[chunks + ch])
        copy.start()
        out_copies.append(copy)
        sent(copies)
    for copy in out_copies:
        copy.wait()


def on_device(
    shared_sizes,
    stiffness,
    load_cases,
    schur_blocks,
    neumann_inverse,
    coarse_basis,
    coarse_dofs,
    coarse_inverse,
):
    groups, subs = lax.axis_size("group"), lax.axis_size("sub")
    nx = math.isqrt(subs)
    nz, ny = subs // nx, groups // CORES
    half = nz // CORES
    unknowns, cases = load_cases.shape[2:]
    chunks = cases // COLS
    ncl = coarse_basis.shape[2]
    own_rows, order = coarse_inverse.shape
    wide, tall = CORES * nx * ncl, ny * nz * ncl

    dma = pltpu.SemaphoreType.DMA
    vmem = pltpu.VMEM
    scratch = [
        vmem((unknowns, unknowns), BF16),
        vmem((unknowns, unknowns), BF16),
        vmem((ncl, unknowns), BF16),
        vmem((own_rows, order), F32),
        vmem((2 * own_rows, order), BF16),
        vmem((chunks, unknowns, COLS), F32),
        vmem((chunks, unknowns, COLS), F32),
        vmem((chunks, unknowns, COLS), F32),
        vmem((chunks, unknowns, COLS), F32),
        vmem((chunks, unknowns, COLS), BF16),
        vmem((unknowns, COLS), BF16),
        vmem((chunks, SH, COLS), F32),
        vmem((chunks, SH, COLS), F32),
        vmem((chunks, SH, COLS), F32),
        vmem((chunks, SH, COLS), F32),
        vmem((SH, COLS), F32),
        vmem((SH, COLS), F32),
        vmem((SH, SH), BF16),
        vmem((SH, SH), BF16),
        vmem((2, ncl, SH), F32),
        vmem((2, ncl, SH), F32),
        vmem((COLS, unknowns), F32),
        vmem((unknowns, 2 * COLS), BF16),
        vmem((tall, order), BF16),
        vmem((order, wide), BF16),
        vmem((nz, own_rows, wide), F32),
        vmem((CORES, nx, half, own_rows, wide), F32),
        vmem((order, 2 * wide), BF16),
        vmem((tall, 3 * wide), BF16),
        vmem((tall, 2 * wide), F32),
        vmem((ITERS, chunks, CORES, nx, ncl, COLS), F32),
        vmem((chunks, ny, nz * ncl, COLS), F32),
        vmem((ITERS, chunks, ny - 1, nz * ncl, COLS), F32),
        vmem((chunks, nz, ncl, COLS), F32),
        vmem((ITERS, chunks, nz, ncl, COLS), F32),
        vmem((ITERS, chunks, 2, nz, ncl, COLS), F32),
        vmem((8, COLS), F32),
        vmem((nz, CORES, nx, 8, COLS), F32),
        vmem((ny, nz, 8, COLS), F32),
        vmem((2, 8, COLS), F32),
        dma((chunks + 4,)),
        dma((2 * chunks,)),
        dma((chunks, 2)), dma((chunks, 2)),
        dma((chunks, 2)), dma((chunks, 2)),
        dma((chunks, 2, nz)), dma((ITERS, chunks, 2, nz)),
        dma((chunks, nx - 1)), dma((ITERS, chunks, nx - 1)),
        dma((chunks,)), dma((ITERS, chunks)),
        dma((chunks, ny - 1)), dma((ITERS, chunks, ny - 1)),
        dma((chunks, nz - 1)), dma((ITERS, chunks, nz - 1)),
        dma((nz - 1,)), dma((nz - 1,)),
        dma((nx - 1, half)), dma((nx - 1, half)),
        dma((nx,)), dma((nx,)),
        dma((2,)), dma((2,)),
        dma((nx - 1,)), dma((nx - 1,)),
        dma((1,)), dma((1,)),
        dma((nz - 1,)), dma((nz - 1,)),
        dma((nz - 1,)), dma((nz - 1,)),
        dma((ny - 1,)), dma((ny - 1,)),
        dma((2,)), dma((2,)),
    ]
    anywhere = pl.BlockSpec(memory_space=pl.ANY)
    out = jax.ShapeDtypeStruct((unknowns, cases), F32)
    sol, res = pl.pallas_call(
        functools.partial(kernel, nx, nz, ny, chunks),
        out_shape=(out, out),
        in_specs=[pl.BlockSpec(memory_space=pltpu.SMEM)] * 2
        + [pl.BlockSpec(memory_space=pltpu.VMEM)]
        + [anywhere] * 5,
        out_specs=(anywhere, anywhere),
        scratch_shapes=scratch,
        compiler_params=pltpu.CompilerParams(
            collective_id=0, has_side_effects=True, vmem_limit_bytes=56 * 1024 * 1024
        ),
        cost_estimate=pl.CostEstimate(flops=2 * 9 * unknowns * unknowns * cases, bytes_accessed=1 << 24, transcendentals=0),
    )(
        shared_sizes[0, 0],
        stiffness[0],
        coarse_dofs[0],
        load_cases[0, 0],
        schur_blocks[0, 0],
        neumann_inverse[0, 0],
        coarse_basis[0, 0],
        coarse_inverse,
    )
    return (sol[None, None], res[None, None])


def solution(mesh):
    return jax.shard_map(
        on_device,
        mesh=mesh,
        in_specs=(
            P("group", "sub", None),
            P("group", "sub"),
            P("group", "sub", None, None),
            P("group", "sub", None, None),
            P("group", "sub", None, None),
            P("group", "sub", None, None),
            P("group", "sub", None),
            P("sub", None),
        ),
        out_specs=(P("group", "sub", None, None), P("group", "sub", None, None)),
        check_vma=False,
    )
```

```python
import functools
import math

import jax
import jax.numpy as jnp
from jax import lax
from jax.experimental import pallas as pl
from jax.experimental.pallas import tpu as pltpu
from jax.sharding import PartitionSpec as P

ITERS = 4
OMEGA = 0.6
SH = 256
COLS = 128
CORES = 2
F32 = jnp.float32
BF16 = jnp.bfloat16


def iota(shape, dim):
    return lax.broadcasted_iota(jnp.int32, shape, dim)


def kernel(
    nx, nz, ny, chunks,
    share, stiff, dofs, loads_hbm, schur_hbm, neumann_hbm, basis_hbm, coarse_hbm,
    sol_hbm, res_hbm,
    schur, neumann, basis, coarse, halves,
    loads, local, field, sol, weighted, rounded,
    from_lower, from_upper, corr_lower, corr_upper,
    weight_head, weight_tail, perm, perm_t,
    edge_out, edge_in, extended, extended_t,
    pick_rows, select, chosen, columns, columns_hl, coarse_k, coarse_part,
    terms, part_y, got_y, part_z, got_z, near_z,
    facts, facts_near, facts_far, facts_side,
    loc_sem, out_sem,
    h1s, h1r, h2s, h2r, nps, npr, xs, xr, cs, cr, ys, yr, zs, zr,
    gzs, gzr, gxs, gxr, gcs, gcr, bs, br,
    fxs, fxr, fcs, fcr, fzs, fzr, fbs, fbr, fys, fyr, fns, fnr,
):
    half = nz // CORES
    subs = nx * nz
    unknowns = loads.shape[1]
    ncl = basis.shape[0]
    order = coarse.shape[1]
    own_rows = coarse.shape[0]
    tail0 = unknowns - SH
    tiles = unknowns // SH
    edges = (0, tiles - 1)
    inner = tuple(range(1, tiles - 1))

    g, s = lax.axis_index("group"), lax.axis_index("sub")
    y, c = g // CORES, g % CORES
    z, x = s // nx, s % nx
    upper = (g, lax.rem(s + 1, subs))
    lower = (g, lax.rem(s + subs - 1, subs))
    x_peers = [(g, z * nx + lax.rem(x + d, nx)) for d in range(1, nx)]
    z_peers = [(g, lax.rem(z + d, nz) * nx + x) for d in range(1, nz)]
    in_column = [lax.rem(z + d, nz) * nx + x for d in range(nz)]
    beside = [[(g, lax.rem(sub + step, subs)) for sub in in_column] for step in (1, subs - 1)]
    y_peers = [(lax.rem(y + d, ny) * CORES + c, s) for d in range(1, ny)]
    core_peer = (y * CORES + 1 - c, s)

    share_low, share_up = share[0], share[1]

    def remote(src, dst, send, recv, to):
        return pltpu.make_async_remote_copy(
            src_ref=src, dst_ref=dst, send_sem=send, recv_sem=recv,
            device_id=to, device_id_type=pl.DeviceIdType.MESH,
        )

    def start(copies):
        for copy in copies:
            copy.start()

    def landed(copies):
        for copy in copies:
            copy.wait_recv()

    def sent(copies):
        for copy in copies:
            copy.wait_send()

    def rows(tile):
        return pl.ds(tile * SH, SH)

    def halo_local(ch):
        return (
            remote(local.at[ch, pl.ds(tail0, SH)], from_lower.at[ch], h1s.at[ch, 0], h1r.at[ch, 0], upper),
            remote(local.at[ch, pl.ds(0, SH)], from_upper.at[ch], h1s.at[ch, 1], h1r.at[ch, 1], lower),
        )

    def halo_field(ch):
        return (
            remote(field.at[ch, pl.ds(tail0, SH)], corr_lower.at[ch], h2s.at[ch, 0], h2r.at[ch, 0], upper),
            remote(field.at[ch, pl.ds(0, SH)], corr_upper.at[ch], h2s.at[ch, 1], h2r.at[ch, 1], lower),
        )

    def terms_x(k, ch):
        own = terms.at[k, ch, c, x]
        return [remote(own, own, xs.at[ch, d], xr.at[k, ch, d], to) for d, to in enumerate(x_peers)]

    def terms_core(k, ch):
        own = terms.at[k, ch, c]
        return (remote(own, own, cs.at[ch], cr.at[k, ch], core_peer),)

    def parts_y(k, ch):
        return [
            remote(part_y.at[ch, lax.rem(y + d + 1, ny)], got_y.at[k, ch, d], ys.at[ch, d], yr.at[k, ch, d], to)
            for d, to in enumerate(y_peers)
        ]

    def parts_z(k, ch):
        return [
            remote(part_z.at[ch, lax.rem(z + d + 1, nz)], got_z.at[k, ch, z], zs.at[ch, d], zr.at[k, ch, d], to)
            for d, to in enumerate(z_peers)
        ]

    def parts_beside(k, ch):
        return [
            remote(
                part_z.at[ch, lax.rem(z + d, nz)], near_z.at[k, ch, side, z],
                nps.at[ch, side, d], npr.at[k, ch, side, d], beside[side][d],
            )
            for side in range(2)
            for d in range(nz)
        ]

    def basis_halo():
        return (
            remote(edge_out.at[0], edge_in.at[0], bs.at[0], br.at[0], upper),
            remote(edge_out.at[1], edge_in.at[1], bs.at[1], br.at[1], lower),
        )

    def columns_z():
        return [
            remote(chosen.at[lax.rem(z + d + 1, nz)], columns.at[c, x, lax.rem(z, half)], gzs.at[d], gzr.at[d], to)
            for d, to in enumerate(z_peers)
        ]

    def columns_x(i):
        own = columns.at[c, x, i]
        return [remote(own, own, gxs.at[d, i], gxr.at[d, i], to) for d, to in enumerate(x_peers)]

    def columns_core(j):
        own = columns.at[c, lax.rem(x + nx - j, nx)]
        return remote(own, own, gcs.at[j], gcr.at[j], core_peer)

    def facts_x():
        own = facts_near.at[z, c, x]
        return [remote(facts, own, fxs.at[d], fxr.at[d], to) for d, to in enumerate(x_peers)]

    def facts_core():
        own = facts_near.at[z, c]
        return (remote(own, own, fcs.at[0], fcr.at[0], core_peer),)

    def facts_z():
        own = facts_near.at[z]
        return [remote(own, own, fzs.at[d], fzr.at[d], to) for d, to in enumerate(z_peers)]

    def far_z():
        return [remote(facts, facts_far.at[y, z], fbs.at[d], fbr.at[d], to) for d, to in enumerate(z_peers)]

    def far_y():
        own = facts_far.at[y]
        return [remote(own, own, fys.at[d], fyr.at[d], to) for d, to in enumerate(y_peers)]

    def facts_beside():
        return (
            remote(facts, facts_side.at[0], fns.at[0], fnr.at[0], upper),
            remote(facts, facts_side.at[1], fns.at[1], fnr.at[1], lower),
        )

    load_in = [
        pltpu.make_async_copy(loads_hbm.at[:, pl.ds(ch * COLS, COLS)], loads.at[ch], loc_sem.at[ch])
        for ch in range(chunks)
    ]
    others = [
        pltpu.make_async_copy(src, dst, loc_sem.at[chunks + i])
        for i, (src, dst) in enumerate(
            ((basis_hbm, basis), (coarse_hbm, coarse), (neumann_hbm, neumann), (schur_hbm, schur))
        )
    ]
    start(load_in)
    start(others)
    facts[...] = jnp.full(facts.shape, stiff[0], F32)
    facts[0:1, :ncl] = dofs[...].astype(F32)
    facts_near[z, c, x] = facts[...]
    facts_far[y, z] = facts[...]
    barrier = pltpu.get_barrier_semaphore()
    peers = [*beside[0], *beside[1], *x_peers, *z_peers, *y_peers, core_peer]
    for peer in peers:
        pl.semaphore_signal(barrier, inc=1, device_id=peer, device_id_type=pl.DeviceIdType.MESH)

    turn = lax.rem(share_up, SH)
    turn_back = lax.rem(2 * SH - share_up, SH)
    moved = (iota((SH, SH), 0) + (SH - share_up)) & (SH - 1)
    perm[...] = jnp.where(iota((SH, SH), 1) == moved, 1.0, 0.0).astype(BF16)
    moved_lane = (iota((SH, SH), 1) + (SH - share_up)) & (SH - 1)
    perm_t[...] = jnp.where(iota((SH, SH), 0) == moved_lane, 1.0, 0.0).astype(BF16)
    for ch in range(chunks):
        load_in[ch].wait()
        loads[ch, tail0:, :] = pltpu.roll(loads[ch, tail0:, :], turn, axis=0)
        local[ch, :, :] = loads[ch, :, :]
    others[1].wait()
    high = coarse[...].astype(BF16)
    halves[0:own_rows, :] = high
    halves[own_rows:, :] = (coarse[...] - high.astype(F32)).astype(BF16)

    pl.semaphore_wait(barrier, len(peers))
    start(facts_x())
    start(facts_beside())
    start(far_z())
    for ch in range(chunks):
        start(halo_local(ch))

    landed(facts_x())
    start(facts_core())
    landed(facts_core())
    start(facts_z())
    landed(far_z())
    start(far_y())
    landed(facts_beside())
    own_stiff = facts[1:2, 0:1]
    low_stiff = facts_side[0, 1:2, 0:1]
    up_stiff = facts_side[1, 1:2, 0:1]
    w_low = own_stiff / (own_stiff + low_stiff)
    w_up = own_stiff / (own_stiff + up_stiff)
    n_low = low_stiff / (low_stiff + own_stiff)
    n_up = up_stiff / (up_stiff + own_stiff)
    in_low = iota((SH, COLS), 0) < share_low
    in_up = iota((SH, COLS), 0) < share_up
    weight_head[...] = jnp.where(in_low, w_low, 1.0)
    weight_tail[...] = jnp.where(in_up, w_up, 1.0)

    others[0].wait()
    basis_tail = jnp.dot(basis[:, tail0:], perm_t[...], preferred_element_type=F32)
    basis[:, tail0:] = basis_tail.astype(BF16)
    edge_out[0] = basis_tail
    edge_out[1] = basis[:, :SH].astype(F32)
    start(basis_halo())
    lane_low = iota((ncl, SH), 1) < share_low
    lane_up = iota((ncl, SH), 1) < share_up
    extended[...] = jnp.zeros_like(extended)
    extended[0:ncl, :] = basis[...].astype(F32)
    extended[0:ncl, :SH] = jnp.where(lane_low, w_low, 1.0) * extended[0:ncl, :SH]
    extended[0:ncl, tail0:] = jnp.where(lane_up, w_up, 1.0) * extended[0:ncl, tail0:]

    def dof_column(row):
        row = jnp.broadcast_to(row, (ncl, COLS))
        hit = iota((ncl, COLS), 0) == iota((ncl, COLS), 1)
        return jnp.sum(jnp.where(hit, row, 0.0), axis=1, keepdims=True).astype(jnp.int32)


    def choose(zt):
        row = jnp.concatenate(
            [facts_near[zt, cc, xx, 0:1, :ncl] for cc in range(CORES) for xx in range(nx)], axis=1
        ).astype(jnp.int32)

        def hot(part, carry):
            at = pl.ds(pl.multiple_of(part * SH, SH), SH)
            index = iota((SH, row.shape[1]), 0) + part * SH
            select[at, :] = jnp.where(index == row, 1.0, 0.0).astype(BF16)
            return carry

        lax.fori_loop(0, order // SH, hot, 0)
        both = jnp.dot(halves[...], select[...], preferred_element_type=F32)
        chosen[zt] = both[:own_rows] + both[own_rows:]

    sends_here = z // half == c
    choose(z)

    @pl.when(sends_here)
    def _():
        columns[c, x, lax.rem(z, half)] = chosen[z]
        start(columns_x(lax.rem(z, half)))

    landed(facts_z())
    for d, copy in enumerate(columns_z()):
        choose(lax.rem(z + d + 1, nz))
        pl.when(sends_here)(copy.start)

    edge = basis_halo()
    landed(edge)
    extended[ncl : 2 * ncl, :SH] = jnp.where(lane_low, n_low * edge_in[0], 0.0)
    extended[2 * ncl : 3 * ncl, tail0:] = jnp.where(lane_up, n_up * edge_in[1], 0.0)
    low = extended[...] - extended[...].astype(BF16).astype(F32)
    extended_t[:, :COLS] = extended[...].T.astype(BF16)
    extended_t[:, COLS:] = low.T.astype(BF16)
    sent(edge)
    landed(far_y())
    for yy in range(ny):
        for zz in range(nz):
            column = jnp.broadcast_to(dof_column(facts_far[yy, zz, 0:1, :]), (ncl, order))
            at = (yy * nz + zz) * ncl
            pick_rows[at : at + ncl, :] = jnp.where(iota((ncl, order), 1) == column, 1.0, 0.0).astype(BF16)

    def align(matrix):
        wide = jnp.dot(perm[...], matrix[tail0:, :], preferred_element_type=F32)
        matrix[tail0:, :] = wide.astype(BF16)

        def turn_columns(tile, carry):
            at = pl.ds(pl.multiple_of(tile * SH, SH), SH)
            swapped = jnp.dot(matrix[at, tail0:], perm_t[...], preferred_element_type=F32)
            matrix[at, tail0:] = swapped.astype(BF16)
            return carry

        lax.fori_loop(0, tiles, turn_columns, 0)

    others[2].wait()
    align(neumann)

    for d, copy in enumerate(columns_z()):
        sender = lax.rem(z + nz - 1 - d, nz)
        pl.when(sender // half == c)(copy.wait_recv)
    for i in range(half):
        pl.when(c * half + i != z)(functools.partial(lambda i: start(columns_x(i)), i))
    columns_core(0).start()

    others[3].wait()
    align(schur)

    @pl.when(sends_here)
    def _():
        sent(columns_z())

    sol[...] = jnp.zeros_like(sol)
    for copies in (facts_beside(), facts_x(), far_z(), facts_core(), far_y(), facts_z()):
        sent(copies)

    def weigh(k, ch):
        landed(halo_local(ch))
        head = local[ch, :SH, :] + jnp.where(in_low, from_lower[ch], 0.0)
        weighted[ch, :SH, :] = (weight_head[...] * head).astype(BF16)
        weighted[ch, SH:tail0, :] = local[ch, SH:tail0, :].astype(BF16)
        tail = local[ch, tail0:, :] + jnp.where(in_up, from_upper[ch], 0.0)
        weighted[ch, tail0:, :] = (weight_tail[...] * tail).astype(BF16)
        terms[k, ch, c, x] = jnp.dot(basis[...], weighted[ch], preferred_element_type=F32)
        start(terms_x(k, ch))

    def precondition(k, ch):
        for tile in edges + inner:
            product = jnp.dot(neumann[rows(tile), :], weighted[ch], preferred_element_type=F32)
            if tile == 0:
                product = weight_head[...] * product
            if tile == tiles - 1:
                product = weight_tail[...] * product
            field[ch, rows(tile), :] = product
            if tile == edges[-1]:
                start(halo_field(ch))

    def to_core(k, ch):
        landed(terms_x(k, ch))
        start(terms_core(k, ch))

    def solve(k, ch):
        landed(terms_core(k, ch))
        mine = terms[k, ch].reshape(CORES * nx * ncl, COLS)
        high = mine.astype(BF16)
        low = (mine - high.astype(F32)).astype(BF16)
        both = jnp.concatenate([high, low], axis=1)
        pair = jnp.dot(coarse_k[:, :wide], both, preferred_element_type=F32)
        rest = jnp.dot(coarse_k[:, wide:], high, preferred_element_type=F32)
        solved = pair[:, :COLS] + (pair[:, COLS:] + rest)
        part_y[ch] = solved.reshape(ny, nz * ncl, COLS)
        start(parts_y(k, ch))

    def sum_y(k, ch):
        copies = parts_y(k, ch)
        landed(copies)
        whole = part_y[ch, y]
        for d in range(ny - 1):
            whole = whole + got_y[k, ch, d]
        part_z[ch] = whole.reshape(nz, ncl, COLS)
        got_z[k, ch, z] = part_z[ch, z]
        start(parts_z(k, ch) + parts_beside(k, ch))
        sent(copies)

    def total(parts):
        result = parts[0]
        for i in range(1, nz):
            result = result + parts[i]
        return result

    def advance(k, ch):
        parts = parts_z(k, ch) + parts_beside(k, ch)
        landed(parts)
        halo = halo_field(ch)
        landed(halo)
        stacked = jnp.concatenate(
            [total(got_z.at[k, ch]), total(near_z.at[k, ch, 0]), total(near_z.at[k, ch, 1]), jnp.zeros((COLS - 3 * ncl, COLS), F32)], axis=0
        ).astype(BF16)
        stacked = jnp.concatenate([stacked, stacked], axis=0)
        sent(parts)
        sent(halo)
        for tile in range(tiles):
            change = field[ch, rows(tile), :] + jnp.dot(
                extended_t[rows(tile), :], stacked, preferred_element_type=F32
            )
            if tile == 0:
                change = change + jnp.where(in_low, corr_lower[ch], 0.0)
            if tile == tiles - 1:
                change = change + jnp.where(in_up, corr_upper[ch], 0.0)
            new = sol[ch, rows(tile), :] + OMEGA * change
            sol[ch, rows(tile), :] = new
            rounded[rows(tile), :] = new.astype(BF16)
        out = halo_local(ch)
        sent(out)
        for tile in edges + inner:
            product = jnp.dot(schur[rows(tile), :], rounded[...], preferred_element_type=F32)
            local[ch, rows(tile), :] = loads[ch, rows(tile), :] - product
            if tile == edges[-1]:
                start(out)
        sent(terms_x(k, ch))
        sent(terms_core(k, ch))

    wide = CORES * nx * ncl
    depth = nx * half * own_rows

    def split_slot(cc, slot):
        for i in range(half):
            block = columns[cc, slot, i]
            high = block.astype(BF16)
            at = pl.ds(pl.multiple_of(((cc * half + i) * nx + slot) * own_rows, own_rows), own_rows)
            columns_hl[at, :wide] = high
            columns_hl[at, wide:] = (block - high.astype(F32)).astype(BF16)

    def pick_half(cc, finish):
        step = min(SH, pick_rows.shape[0])
        inside = pl.ds(pl.multiple_of(cc * depth, depth), depth)

        def row_tile(tile, carry):
            at = pl.ds(pl.multiple_of(tile * step, step), step)
            both = jnp.dot(pick_rows[at, inside], columns_hl[inside, :], preferred_element_type=F32)
            if not finish:
                coarse_part[at, :] = both
                return carry
            both = both + coarse_part[at, :]
            coarse_k[at, :wide] = both[:, :wide].astype(BF16)
            coarse_k[at, wide:] = both[:, wide:].astype(BF16)
            return carry

        lax.fori_loop(0, pick_rows.shape[0] // step, row_tile, 0)

    def finish_setup():
        to_peer = [columns_core(j) for j in range(nx)]
        split_slot(c, x)
        pieces = [columns_x(i) for i in range(half)]
        for d in range(nx - 1):
            landed([piece[d] for piece in pieces])
            to_peer[d + 1].start()
            split_slot(c, lax.rem(x + nx - d - 1, nx))
        pick_half(c, False)
        landed(to_peer)
        for slot in range(nx):
            split_slot(1 - c, slot)
        pick_half(1 - c, True)
        for piece in pieces:
            sent(piece)
        sent(to_peer)

    def each_chunk(step):
        def body(ch, carry):
            step(0, ch)
            return carry

        lax.fori_loop(0, chunks, body, 0)

    lanes = chunks + 2

    def tick(now, carry):
        def run(step, late, first=0):
            turn = now - late

            @pl.when((turn >= first * lanes) & (turn < ITERS * lanes) & (lax.rem(turn + lanes, lanes) < chunks))
            def _():
                step(turn // lanes, lax.rem(turn, lanes))

        run(weigh, 0, 1)
        run(to_core, 1, 1)
        run(sum_y, 2)
        run(solve, 1)
        run(precondition, 0, 1)
        run(advance, 3)
        return carry

    each_chunk(weigh)
    each_chunk(precondition)
    each_chunk(to_core)
    finish_setup()
    lax.fori_loop(1, ITERS * lanes + 3 - 1, tick, 0)

    out_copies = []
    for ch in range(chunks):
        sol[ch, tail0:, :] = pltpu.roll(sol[ch, tail0:, :], turn_back, axis=0)
        copy = pltpu.make_async_copy(sol.at[ch], sol_hbm.at[:, pl.ds(ch * COLS, COLS)], out_sem.at[ch])
        copy.start()
        out_copies.append(copy)
    for ch in range(chunks):
        copies = halo_local(ch)
        landed(copies)
        field[ch, :SH, :] = local[ch, :SH, :] + jnp.where(in_low, from_lower[ch], 0.0)
        field[ch, SH:tail0, :] = local[ch, SH:tail0, :]
        tail = local[ch, tail0:, :] + jnp.where(in_up, from_upper[ch], 0.0)
        field[ch, tail0:, :] = pltpu.roll(tail, turn_back, axis=0)
        copy = pltpu.make_async_copy(field.at[ch], res_hbm.at[:, pl.ds(ch * COLS, COLS)], out_sem.at[chunks + ch])
        copy.start()
        out_copies.append(copy)
        sent(copies)
    for copy in out_copies:
        copy.wait()


def on_device(
    shared_sizes,
    stiffness,
    load_cases,
    schur_blocks,
    neumann_inverse,
    coarse_basis,
    coarse_dofs,
    coarse_inverse,
):
    groups, subs = lax.axis_size("group"), lax.axis_size("sub")
    nx = math.isqrt(subs)
    nz, ny = subs // nx, groups // CORES
    half = nz // CORES
    unknowns, cases = load_cases.shape[2:]
    chunks = cases // COLS
    ncl = coarse_basis.shape[2]
    own_rows, order = coarse_inverse.shape
    wide, tall = CORES * nx * ncl, ny * nz * ncl

    dma = pltpu.SemaphoreType.DMA
    vmem = pltpu.VMEM
    scratch = [
        vmem((unknowns, unknowns), BF16),
        vmem((unknowns, unknowns), BF16),
        vmem((ncl, unknowns), BF16),
        vmem((own_rows, order), F32),
        vmem((2 * own_rows, order), BF16),
        vmem((chunks, unknowns, COLS), F32),
        vmem((chunks, unknowns, COLS), F32),
        vmem((chunks, unknowns, COLS), F32),
        vmem((chunks, unknowns, COLS), F32),
        vmem((chunks, unknowns, COLS), BF16),
        vmem((unknowns, COLS), BF16),
        vmem((chunks, SH, COLS), F32),
        vmem((chunks, SH, COLS), F32),
        vmem((chunks, SH, COLS), F32),
        vmem((chunks, SH, COLS), F32),
        vmem((SH, COLS), F32),
        vmem((SH, COLS), F32),
        vmem((SH, SH), BF16),
        vmem((SH, SH), BF16),
        vmem((2, ncl, SH), F32),
        vmem((2, ncl, SH), F32),
        vmem((COLS, unknowns), F32),
        vmem((unknowns, 2 * COLS), BF16),
        vmem((tall, order), BF16),
        vmem((order, wide), BF16),
        vmem((nz, own_rows, wide), F32),
        vmem((CORES, nx, half, own_rows, wide), F32),
        vmem((order, 2 * wide), BF16),
        vmem((tall, 2 * wide), BF16),
        vmem((tall, 2 * wide), F32),
        vmem((ITERS, chunks, CORES, nx, ncl, COLS), F32),
        vmem((chunks, ny, nz * ncl, COLS), F32),
        vmem((ITERS, chunks, ny - 1, nz * ncl, COLS), F32),
        vmem((chunks, nz, ncl, COLS), F32),
        vmem((ITERS, chunks, nz, ncl, COLS), F32),
        vmem((ITERS, chunks, 2, nz, ncl, COLS), F32),
        vmem((8, COLS), F32),
        vmem((nz, CORES, nx, 8, COLS), F32),
        vmem((ny, nz, 8, COLS), F32),
        vmem((2, 8, COLS), F32),
        dma((chunks + 4,)),
        dma((2 * chunks,)),
        dma((chunks, 2)), dma((chunks, 2)),
        dma((chunks, 2)), dma((chunks, 2)),
        dma((chunks, 2, nz)), dma((ITERS, chunks, 2, nz)),
        dma((chunks, nx - 1)), dma((ITERS, chunks, nx - 1)),
        dma((chunks,)), dma((ITERS, chunks)),
        dma((chunks, ny - 1)), dma((ITERS, chunks, ny - 1)),
        dma((chunks, nz - 1)), dma((ITERS, chunks, nz - 1)),
        dma((nz - 1,)), dma((nz - 1,)),
        dma((nx - 1, half)), dma((nx - 1, half)),
        dma((nx,)), dma((nx,)),
        dma((2,)), dma((2,)),
        dma((nx - 1,)), dma((nx - 1,)),
        dma((1,)), dma((1,)),
        dma((nz - 1,)), dma((nz - 1,)),
        dma((nz - 1,)), dma((nz - 1,)),
        dma((ny - 1,)), dma((ny - 1,)),
        dma((2,)), dma((2,)),
    ]
    anywhere = pl.BlockSpec(memory_space=pl.ANY)
    out = jax.ShapeDtypeStruct((unknowns, cases), F32)
    sol, res = pl.pallas_call(
        functools.partial(kernel, nx, nz, ny, chunks),
        out_shape=(out, out),
        in_specs=[pl.BlockSpec(memory_space=pltpu.SMEM)] * 2
        + [pl.BlockSpec(memory_space=pltpu.VMEM)]
        + [anywhere] * 5,
        out_specs=(anywhere, anywhere),
        scratch_shapes=scratch,
        compiler_params=pltpu.CompilerParams(
            collective_id=0, has_side_effects=True, vmem_limit_bytes=56 * 1024 * 1024
        ),
        cost_estimate=pl.CostEstimate(flops=2 * 9 * unknowns * unknowns * cases, bytes_accessed=1 << 24, transcendentals=0),
    )(
        shared_sizes[0, 0],
        stiffness[0],
        coarse_dofs[0],
        load_cases[0, 0],
        schur_blocks[0, 0],
        neumann_inverse[0, 0],
        coarse_basis[0, 0],
        coarse_inverse,
    )
    return (sol[None, None], res[None, None])


def solution(mesh):
    return jax.shard_map(
        on_device,
        mesh=mesh,
        in_specs=(
            P("group", "sub", None),
            P("group", "sub"),
            P("group", "sub", None, None),
            P("group", "sub", None, None),
            P("group", "sub", None, None),
            P("group", "sub", None, None),
            P("group", "sub", None),
            P("sub", None),
        ),
        out_specs=(P("group", "sub", None, None), P("group", "sub", None, None)),
        check_vma=False,
    )
```
